32 devices in a mesh: groups: 2 (over y), comp: 4 (over x, core), expert: 4 (over z).
Axes of the slice: x: 2, y: 2, z: 4, core: 2. Of those that a mesh axis runs over, the one named last changes fastest.
Arguments:
- states: bfloat16 [4, 768, 3072], P('comp', ('groups', 'expert')), parts along dimension 1, may hold values from -9 to 9
- routes: int32 [4, 768, 2], P('comp', ('groups', 'expert')), parts along dimension 1, may hold values from 0 to 3, as said below
- slots: int32 [4, 768, 2], P('comp', ('groups', 'expert')), parts along dimension 1, may hold values from 0 to 71, as said below
- timesteps: int32 [8], P(('groups', 'comp')), parts along dimension 0, may hold values from 0 to 49
- router_weight: bfloat16 [4, 3072, 4], P('comp'), may hold values from -0.109375 to 0.109375
- expert_in: bfloat16 [4, 3072, 8192], P('comp', None, 'expert'), may hold values from -0.109375 to 0.109375
- expert_out: bfloat16 [4, 8192, 3072], P('comp', 'expert'), may hold values from -0.125 to 0.125
- modulation: bfloat16 [50, 3, 3072], replicated, may hold values from -2 to 2
Outputs:
- new_states: bfloat16 [4, 768, 3072], P('comp', ('groups', 'expert')), parts along dimension 1
The draws below stay inside these ranges and needn't reach their ends.
There are 2 independent parts, one for each index of `groups`. The reference program is written for one: setup_inputs(seed, part) draws one part's arguments, and reference() takes and returns one part's arrays. A program takes and returns all parts, laid end to end along the dimension named above; an argument that names none is the same for every part. Nothing has to cross between parts.
Inputs may be any that keep to these rules, and one draw needn't show every extreme that they name: `routes`: in every aligned block of 96 tokens a token's two experts differ, each expert is named by at most 72 tokens, and in each component one expert is named by exactly 72 tokens of every block. Within one block and one expert the slots of the routes to it are distinct and numbered from 0 in token order.
All inputs are finite; a program needn't handle non-finite values.
Results may differ from the reference program's by a relative error of at most 0.0043.
Values may be sent and summed in bfloat16 or wider, within the bound.
No kernel may reach another device: no remote copies, remote signals or barrier semaphores. Data moves between devices by JAX's collectives and lax.ppermute only.
A program may use at most 128 MiB of HBM per device.

```python
import math
import jax
import jax.numpy as jnp
from jax import lax

D = 3072
HID = 2048
EXPERTS = 4
STEPS = 50
TOK_DEV = 96
COMP = 4
TOKENS = 384
SHARDS = 1
MOST = 72
N_EXPERT = 4


def route_table(key):
    blocks = TOKENS // TOK_DEV
    keys = jax.random.split(key, 5)
    shape = (COMP, blocks, TOK_DEV)
    hot = jax.random.randint(keys[0], (COMP, 1, 1), 0, EXPERTS)
    scores = jax.random.randint(keys[1], shape, 0, 1 << 20) * TOK_DEV + jnp.arange(TOK_DEV, dtype=jnp.int32)
    order = jnp.argsort(scores, axis=-1)
    rank = jnp.argsort(order, axis=-1).astype(jnp.int32)
    is_hot = rank < MOST
    paired = (hot + 1 + rank % (EXPERTS - 1)) % EXPERTS
    first_pick = jax.random.randint(keys[2], shape, 0, EXPERTS - 1)
    offset = jax.random.randint(keys[3], shape, 0, EXPERTS - 2)
    cold_one = (hot + 1 + first_pick) % EXPERTS
    cold_two = (hot + 1 + (first_pick + 1 + offset) % (EXPERTS - 1)) % EXPERTS
    one = jnp.where(is_hot, hot, cold_one)
    two = jnp.where(is_hot, paired, cold_two)
    flip = jax.random.randint(keys[4], shape, 0, 2)
    left = jnp.where(flip == 1, two, one)
    right = jnp.where(flip == 1, one, two)
    chosen = jnp.stack([left, right], axis=-1).astype(jnp.int32)
    onehot = (chosen[..., None] == jnp.arange(EXPERTS, dtype=jnp.int32)).astype(jnp.int32)
    per_token = jnp.sum(onehot, axis=3)
    before = jnp.cumsum(per_token, axis=2) - per_token
    places = jnp.sum(onehot * before[:, :, :, None, :], axis=-1)
    return (chosen.reshape(COMP, TOKENS, 2), places.reshape(COMP, TOKENS, 2).astype(jnp.int32))


def draw_routes(key, part):
    return route_table(key)[0]


def draw_slots(key, part):
    return route_table(key)[1]


def draw_states(key, part):
    key = jax.random.fold_in(key, 11)
    keys = jax.random.split(key, 2)
    rows = jnp.exp(jax.random.uniform(keys[0], (COMP, TOKENS, 1), jnp.float32, math.log(0.3), math.log(3.0)))
    base = jnp.clip(jax.random.normal(keys[1], (COMP, TOKENS, D), jnp.float32), -3.0, 3.0)
    return (base * rows).astype(jnp.bfloat16)


def set_ends(entries, own_key, smallest, high):
    longest = entries.shape.index(max(entries.shape))
    spots = []
    for shift in (0, 1):
        where = [jax.random.randint(jax.random.fold_in(own_key, axis), (), 0, length) for axis, length in enumerate(entries.shape)]
        where[longest] = (where[longest] + shift) % entries.shape[longest]
        spots.append(tuple(where))
    return entries.at[spots[0]].set(smallest).at[spots[1]].set(high)


def shard_levels(stream_key, extent, cuts, low, largest):
    factor_of = 1.0
    for dim, shards_of in cuts:
        steps = jax.random.uniform(jax.random.fold_in(jax.random.fold_in(stream_key, 6), dim), (shards_of,), jnp.float32, low / len(cuts), largest / len(cuts))
        factor_of = factor_of * jnp.repeat(jnp.exp(steps), extent[dim] // shards_of).reshape((-1,) + (1,) * (len(extent) - 1 - dim))
    return factor_of


def gaussian(key, extent, scale, limit, shards=(), kind=jnp.bfloat16):
    values = jax.random.normal(key, extent, jnp.float32) * scale
    if len(shards) > 0:
        values = shard_levels(key, extent, shards, -0.22, 0.18) * values
    return jnp.clip(values, min=-limit, max=limit).astype(kind)


def setup_inputs(seed: int = 0, part: int = 0) -> dict:
    streams_of = jax.random.split(jax.random.key(seed), 9)
    own_keys = jax.random.split(jax.random.fold_in(streams_of[8], part), 9)
    states = draw_states(jax.random.fold_in(jax.random.fold_in(streams_of[8], part), 71), part)
    routes = draw_routes(jax.random.fold_in(jax.random.fold_in(streams_of[8], part), 71), part)
    slots = draw_slots(jax.random.fold_in(jax.random.fold_in(streams_of[8], part), 71), part)
    timesteps = set_ends(jax.random.randint(own_keys[3], (COMP,), 0, STEPS), jax.random.fold_in(own_keys[3], 1), 0, STEPS - 1).astype(jnp.int32)
    router_weight = gaussian(streams_of[4], (COMP, D, EXPERTS), D ** -0.5, 0.109375, ((0, 4),))
    expert_in = gaussian(streams_of[5], (COMP, D, EXPERTS * HID), D ** -0.5, 0.109375, ((0, 4), (2, 4)))
    expert_out = gaussian(streams_of[6], (COMP, EXPERTS * HID, D), HID ** -0.5, 0.125, ((0, 4), (1, 4)))
    modulation = gaussian(streams_of[7], (STEPS, 3, D), 0.5, 2.0)
    return dict(states=states, routes=routes, slots=slots, timesteps=timesteps, router_weight=router_weight, expert_in=expert_in, expert_out=expert_out, modulation=modulation)


def modulate(incoming, mod):
    values = incoming.astype(jnp.float32)
    centred = values - lax.optimization_barrier(jnp.mean(values, axis=-1, keepdims=True))
    spread = lax.optimization_barrier(jnp.mean(centred * centred, axis=-1, keepdims=True))
    normed = centred * lax.rsqrt(spread + 1e-06)
    return (normed * (1.0 + mod[0]) + mod[1]).astype(jnp.bfloat16)

def gating(modulated, weight, chosen):
    logits = jnp.dot(modulated, weight, preferred_element_type=jnp.float32)
    picks = chosen[..., None] == jnp.arange(weight.shape[1], dtype=jnp.int32)
    selected = lax.optimization_barrier(jnp.sum(jnp.where(picks, logits[:, None, :], jnp.float32(0.0)), axis=-1))
    sig = jax.nn.sigmoid(selected)
    return sig / lax.optimization_barrier(jnp.sum(sig, axis=1, keepdims=True))

def expert_rows(rows, w_first, w_second):
    hidden = jax.nn.gelu(jnp.dot(rows, w_first, preferred_element_type=jnp.float32), approximate=True).astype(jnp.bfloat16)
    width = HID // SHARDS
    total = jnp.zeros((rows.shape[0], w_second.shape[1]), jnp.float32)
    for shard in range(SHARDS):
        part_sum = jnp.dot(hidden[:, shard * width:(shard + 1) * width], w_second[shard * width:(shard + 1) * width], preferred_element_type=jnp.float32)
        rounded = lax.optimization_barrier(part_sum.astype(jnp.bfloat16))
        total = total + rounded.astype(jnp.float32)
    return total

def apply_expert(packed):
    return expert_rows(packed[0], packed[1], packed[2])

def reference(states, routes, slots, timesteps, router_weight, expert_in, expert_out, modulation):
    source = jnp.arange(TOKENS, dtype=jnp.int32) // TOK_DEV
    results_all = []
    for comp_index in range(COMP):
        incoming = states[(comp_index - 1) % COMP]
        mod = modulation[timesteps[comp_index]].astype(jnp.float32)
        modulated = modulate(incoming, mod)
        chosen = routes[comp_index]
        gates = gating(modulated, router_weight[comp_index], chosen)
        position = (source[:, None] * MOST + slots[comp_index]).astype(jnp.int32)
        buffer = jnp.zeros((EXPERTS, N_EXPERT * MOST, D), jnp.bfloat16)
        buffer = buffer.at[chosen, position].set(jnp.broadcast_to(modulated[:, None, :], (TOKENS, 2, D)))
        w_first = expert_in[comp_index].reshape(D, EXPERTS, HID).transpose(1, 0, 2)
        w_second = expert_out[comp_index].reshape(EXPERTS, HID, D)
        results = lax.map(apply_expert, (buffer, w_first, w_second))
        picked = results[chosen, position]
        mixture = lax.optimization_barrier(jnp.sum(gates[..., None] * picked, axis=1))
        updated = incoming.astype(jnp.float32) + (1.0 + mod[2]) * mixture
        results_all.append(updated.astype(jnp.bfloat16))
    return jnp.stack(results_all)
```

```python
import functools

import jax
import jax.numpy as jnp
from jax import lax
from jax.experimental import pallas as pl
from jax.experimental.pallas import tpu as pltpu
from jax.sharding import PartitionSpec as P

MIB = 1024 * 1024


def shifted(block, axis, distance):
    devices = range(lax.axis_size(axis))
    route = [((i - distance) % len(devices), i) for i in devices]
    return lax.ppermute(block, axis, route)


def swapped(block, mask):
    return lax.ppermute(block, "expert", [(e, e ^ mask) for e in range(lax.axis_size("expert"))])


def advanced(block, mask):
    comps, experts = lax.axis_size("comp"), lax.axis_size("expert")
    route = [
        (c * experts + e, (c + 1) % comps * experts + (e ^ mask))
        for c in range(comps)
        for e in range(experts)
    ]
    return lax.ppermute(block, ("comp", "expert"), route)


def modulate(incoming, scale, shift):
    values = incoming.astype(jnp.float32)
    centred = values - jnp.mean(values, axis=-1, keepdims=True)
    spread = jnp.mean(centred * centred, axis=-1, keepdims=True)
    normed = centred * lax.rsqrt(spread + 1e-06)
    return (normed * (1.0 + scale) + shift).astype(jnp.bfloat16)


def pick_logits(logits, chosen):
    picks = chosen[..., None] == jnp.arange(logits.shape[1], dtype=jnp.int32)
    return jnp.sum(jnp.where(picks, logits[:, None, :], jnp.float32(0.0)), axis=-1)


def gating(modulated, weight, chosen):
    logits = jnp.dot(modulated, weight, preferred_element_type=jnp.float32)
    sig = jax.nn.sigmoid(pick_logits(logits, chosen))
    return sig / jnp.sum(sig, axis=1, keepdims=True)


def slot_rows(chosen, slots, expert, most):
    taken = jnp.where(chosen == expert, slots, -1)
    rows = lax.broadcasted_iota(jnp.int32, (most, chosen.shape[0]), 0)
    return ((rows == taken[None, :, 0]) | (rows == taken[None, :, 1])).astype(jnp.bfloat16)


def select(rows, block):
    return jnp.dot(rows, block, preferred_element_type=jnp.float32).astype(jnp.bfloat16)


def spread_back(rows, result):
    return lax.dot_general(rows, result, (((0,), (0,)), ((), ())), preferred_element_type=jnp.float32)


def tiles(size, step):
    return [(i, min(step, size - i)) for i in range(0, size, step)]


def experts_on(x, w1, w2, hidden, store):
    for start, size in tiles(w1.shape[1], 512):
        value = jnp.dot(x[...], w1[:, start:start + size], preferred_element_type=jnp.float32)
        hidden[:, start:start + size] = jax.nn.gelu(value, approximate=True).astype(jnp.bfloat16)
    for start, size in tiles(w2.shape[1], 512):
        value = jnp.dot(hidden[...], w2[:, start:start + size], preferred_element_type=jnp.float32)
        store(start, size, value)


def near_kernel(most, own, rows, sib, mod, w1, w2, out_own, out_sib, x, hidden):
    pad = x.shape[0] // 2
    x[0:pad, :] = jnp.zeros((pad, x.shape[1]), x.dtype)
    x[pad:2 * pad, :] = jnp.zeros((pad, x.shape[1]), x.dtype)
    x[0:most, :] = select(rows[...], own[...])
    x[pad:pad + most, :] = modulate(sib[...], mod[0:1, :], mod[1:2, :])

    def store(start, size, value):
        out_own[:, start:start + size] = value[0:most].astype(jnp.bfloat16)
        out_sib[:, start:start + size] = value[pad:pad + most].astype(jnp.bfloat16)

    experts_on(x, w1, w2, hidden, store)


def far_kernel(most, cut, first, second, mod, w1, w2, out, raw, x, hidden):
    raw[:, 0:cut] = first[...].astype(jnp.float32)
    raw[:, cut:] = second[...].astype(jnp.float32)
    x[...] = jnp.zeros_like(x)
    x[0:most, :] = modulate(raw[...], mod[0:1, :], mod[1:2, :])

    def store(start, size, value):
        out[:, start:start + size] = value[0:most].astype(jnp.bfloat16)

    experts_on(x, w1, w2, hidden, store)


def cost(rows, width, hid):
    return pl.CostEstimate(
        flops=4 * rows * width * hid, bytes_accessed=4 * rows * width, transcendentals=rows * hid
    )


def params():
    return pltpu.CompilerParams(vmem_limit_bytes=16 * MIB)


def near(own, rows, sib, mod, w1, w2):
    most, width = sib.shape
    pad = -(-most // 16) * 16
    hid = w1.shape[1]
    vmem = pl.BlockSpec(memory_space=pltpu.VMEM)
    shape = jax.ShapeDtypeStruct((most, width), jnp.bfloat16)
    return pl.pallas_call(
        functools.partial(near_kernel, most),
        out_shape=(shape, shape),
        in_specs=[vmem] * 6,
        out_specs=(vmem, vmem),
        scratch_shapes=[
            pltpu.VMEM((2 * pad, width), jnp.bfloat16),
            pltpu.VMEM((2 * pad, hid), jnp.bfloat16),
        ],
        compiler_params=params(),
        cost_estimate=cost(2 * most, width, hid),
    )(own, rows, sib, mod, w1, w2)


def far(first, second, mod, w1, w2):
    most, cut = first.shape
    width = cut + second.shape[1]
    pad = -(-most // 16) * 16
    hid = w1.shape[1]
    vmem = pl.BlockSpec(memory_space=pltpu.VMEM)
    return pl.pallas_call(
        functools.partial(far_kernel, most, cut),
        out_shape=jax.ShapeDtypeStruct((most, width), jnp.bfloat16),
        in_specs=[vmem] * 5,
        out_specs=vmem,
        scratch_shapes=[
            pltpu.VMEM((most, width), jnp.float32),
            pltpu.VMEM((pad, width), jnp.bfloat16),
            pltpu.VMEM((pad, hid), jnp.bfloat16),
        ],
        compiler_params=params(),
        cost_estimate=cost(most, width, hid),
    )(first, second, mod, w1, w2)


def quad_body(states, routes, slots, timesteps, router_weight, expert_in, expert_out, modulation):
    source = states[0]
    width = source.shape[1]
    most = 3 * source.shape[0] // 4
    cut = width // 256 * 128
    here = lax.axis_index("expert")
    chosen, places = routes[0], slots[0]
    w1 = pltpu.with_memory_space_constraint(expert_in[0], pltpu.VMEM)
    w2 = pltpu.with_memory_space_constraint(expert_out[0], pltpu.VMEM)

    crossed = advanced(source[:, :cut], 2)
    table = jnp.concatenate([chosen, places], axis=1)
    ahead = shifted(table, "comp", -1)
    incoming = shifted(source, "comp", 1)
    mod = modulation[timesteps[0]].astype(jnp.float32)

    def ahead_rows(mask):
        return slot_rows(ahead[:, :2], ahead[:, 2:], here ^ mask, most)

    sib = advanced(select(ahead_rows(1), source), 1)
    far_x = advanced(select(ahead_rows(2), source[:, cut:]), 2)
    far_z = advanced(select(ahead_rows(3), source[:, cut:]), 3)

    modulated = modulate(incoming, mod[0], mod[1])
    gates = gating(modulated, router_weight[0], chosen)
    packed = jnp.concatenate([table.astype(jnp.float32), gates], axis=1)
    other = swapped(packed, 2)
    x_chosen = other[:, 0:2].astype(jnp.int32)
    x_places = other[:, 2:4].astype(jnp.int32)
    x_gates = other[:, 4:6]

    def gate_of(expert, chosen, gates):
        return jnp.sum(jnp.where(chosen == expert, gates, 0.0), axis=1, keepdims=True)

    rows_x = slot_rows(x_chosen, x_places, here, most)
    rows_r = slot_rows(x_chosen, x_places, here ^ 1, most)
    relayed = swapped(select(rows_r, crossed), 1)

    rows_own = slot_rows(chosen, places, here, most)
    y_own, y_sib = near(modulated, rows_own, sib, mod, w1, w2)
    back_s = swapped(y_sib, 1)
    y_x = far(select(rows_x, crossed), far_x, mod, w1, w2)
    back_x = swapped(y_x[:, cut:], 2)
    y_z = far(relayed, far_z, mod, w1, w2)
    lent = swapped(y_z[:, :cut], 1)
    back_z = swapped(y_z[:, cut:], 3)
    joint = gate_of(here, x_chosen, x_gates) * spread_back(rows_x, y_x[:, :cut])
    joint += gate_of(here ^ 1, x_chosen, x_gates) * spread_back(rows_r, lent)
    back_u = swapped(joint.astype(jnp.bfloat16), 2)

    def mixed(mask, result):
        rows = slot_rows(chosen, places, here ^ mask, most)
        return gate_of(here ^ mask, chosen, gates) * spread_back(rows, result)

    base = mixed(0, y_own) + mixed(1, back_s)
    left = base[:, :cut] + back_u.astype(jnp.float32)
    right = base[:, cut:] + mixed(2, back_x) + mixed(3, back_z)
    mixture = jnp.concatenate([left, right], axis=1)
    updated = incoming.astype(jnp.float32) + (1.0 + mod[2]) * mixture
    return updated.astype(jnp.bfloat16)[None]


def general_body(states, routes, slots, timesteps, router_weight, expert_in, expert_out, modulation):
    devices = lax.axis_size("expert")
    tokens_here = states.shape[1]
    width = states.shape[2]
    experts = router_weight.shape[2]
    shards = devices // experts
    most = 3 * tokens_here // 4
    incoming = shifted(states[0], "comp", 1)
    mod = modulation[timesteps[0]].astype(jnp.float32)
    modulated = modulate(incoming, mod[0], mod[1])
    chosen = routes[0]
    gates = gating(modulated, router_weight[0], chosen)
    target = chosen * most + slots[0]
    place = target[..., None] == jnp.arange(experts * most, dtype=jnp.int32)
    occupied = jnp.any(place, axis=1).astype(jnp.bfloat16)
    buffer = jnp.einsum(
        "tr,td->rd", occupied, modulated, preferred_element_type=jnp.float32
    ).astype(jnp.bfloat16)
    mix_weights = jnp.sum(jnp.where(place, gates[..., None], jnp.float32(0.0)), axis=1)
    w_first = expert_in[0]
    w_second = expert_out[0]
    copies = jnp.broadcast_to(
        buffer.reshape(experts, 1, most, width), (experts, shards, most, width)
    )
    outgoing = copies.reshape(devices, most, width)
    received = lax.all_to_all(outgoing, "expert", split_axis=0, concat_axis=0, tiled=True)
    count = received.shape[1]
    hidden = jax.nn.gelu(
        jnp.dot(received.reshape(-1, width), w_first, preferred_element_type=jnp.float32),
        approximate=True,
    )
    partial_value = (
        jnp.dot(hidden.astype(jnp.bfloat16), w_second, preferred_element_type=jnp.float32)
        .astype(jnp.bfloat16)
        .reshape(devices, count, width)
    )
    returned = lax.all_to_all(partial_value, "expert", split_axis=0, concat_axis=0, tiled=True)
    combined = jnp.sum(returned.reshape(experts, shards, most, width).astype(jnp.float32), axis=1)
    mixture = jnp.dot(
        mix_weights,
        combined.reshape(experts * most, width),
        precision=lax.Precision.HIGHEST,
        preferred_element_type=jnp.float32,
    )
    updated = incoming.astype(jnp.float32) + (1.0 + mod[2]) * mixture
    return updated.astype(jnp.bfloat16)[None]


def body(states, routes, slots, timesteps, router_weight, *rest):
    quad = lax.axis_size("expert") == router_weight.shape[2] == 4
    chosen_body = quad_body if quad else general_body
    return chosen_body(states, routes, slots, timesteps, router_weight, *rest)


def solution(mesh):
    in_specs = (
        P("comp", ("groups", "expert"), None),
        P("comp", ("groups", "expert"), None),
        P("comp", ("groups", "expert"), None),
        P(("groups", "comp")),
        P("comp", None, None),
        P("comp", None, "expert"),
        P("comp", "expert", None),
        P(),
    )
    out_specs = P("comp", ("groups", "expert"), None)
    return jax.shard_map(body, mesh=mesh, in_specs=in_specs, out_specs=out_specs, check_vma=False)
```

```python
import jax
import jax.numpy as jnp
from jax import lax
from jax.experimental import pallas as pl
from jax.experimental.pallas import tpu as pltpu
from jax.sharding import PartitionSpec as P

MIB = 1024 * 1024
VMEM = pl.BlockSpec(memory_space=pltpu.VMEM)
ANY = pl.BlockSpec(memory_space=pl.ANY)
HBM = pl.BlockSpec(memory_space=pltpu.HBM)
PARAMS = pltpu.CompilerParams(vmem_limit_bytes=10 * MIB)


def shifted(block, axis, distance):
    devices = range(lax.axis_size(axis))
    route = [((i - distance) % len(devices), i) for i in devices]
    return lax.ppermute(block, axis, route)


def swapped(block, mask):
    return lax.ppermute(block, "expert", [(e, e ^ mask) for e in range(lax.axis_size("expert"))])


def advanced(block, mask):
    comps, experts = lax.axis_size("comp"), lax.axis_size("expert")
    route = [
        (c * experts + e, (c + 1) % comps * experts + (e ^ mask))
        for c in range(comps)
        for e in range(experts)
    ]
    return lax.ppermute(block, ("comp", "expert"), route)


def modulate(incoming, scale, shift):
    values = incoming.astype(jnp.float32)
    centred = values - jnp.mean(values, axis=-1, keepdims=True)
    spread = jnp.mean(centred * centred, axis=-1, keepdims=True)
    normed = centred * lax.rsqrt(spread + 1e-06)
    return (normed * (1.0 + scale) + shift).astype(jnp.bfloat16)


def slot_rows(target, mask, most):
    rows = lax.broadcasted_iota(jnp.int32, (most, target.shape[1]), 0) + mask * most
    hit = (rows == target[0:1, :]) | (rows == target[1:2, :])
    return jnp.where(hit, 1.0, 0.0).astype(jnp.bfloat16)


def select(rows, block):
    return jnp.dot(rows, block, preferred_element_type=jnp.float32).astype(jnp.bfloat16)


def gate_column(target, gates, mask, most):
    picked = (target >= mask * most) & (target < (mask + 1) * most)
    row = jnp.sum(jnp.where(picked, gates, 0.0), axis=0, keepdims=True)
    size = target.shape[1]
    places = (size, size)
    same = lax.broadcasted_iota(jnp.int32, places, 0) == lax.broadcasted_iota(jnp.int32, places, 1)
    return jnp.sum(jnp.where(same, row, 0.0), axis=1, keepdims=True)


def mixed(target, gates, mask, result):
    rows = slot_rows(target, mask, result.shape[0])
    spread = lax.dot_general(
        rows, result, (((0,), (0,)), ((), ())), preferred_element_type=jnp.float32
    )
    return gate_column(target, gates, mask, result.shape[0]) * spread


def tiles(size, step):
    return [(i, min(step, size - i)) for i in range(0, size, step)]


def first_layer(x, w1, hidden, ready=lambda index: None):
    for index, (start, size) in enumerate(tiles(w1.shape[1], 512)):
        ready(index)
        value = jnp.dot(x[...], w1[:, start:start + size], preferred_element_type=jnp.float32)
        hidden[:, start:start + size] = jax.nn.gelu(value, approximate=True).astype(jnp.bfloat16)


def second_layer(hidden, w2, columns, outs, ready=lambda index: None):
    pad = hidden.shape[0] // len(outs)
    for index, (start, size) in enumerate(tiles(columns[1] - columns[0], 512)):
        ready(index)
        part = w2[:, columns[0] + start:columns[0] + start + size]
        value = jnp.dot(hidden[...], part, preferred_element_type=jnp.float32)
        for i, out in enumerate(outs):
            rows = value[i * pad:i * pad + out.shape[0]]
            out[:, start:start + size] = rows.astype(jnp.bfloat16)


def source_kernel(source, ahead, out_x, out_z, out_s):
    most = out_s.shape[0]
    cut = source.shape[1] - out_x.shape[1]
    out_x[...] = select(slot_rows(ahead[...], 2, most), source[:, cut:])
    out_z[...] = select(slot_rows(ahead[...], 3, most), source[:, cut:])
    out_s[...] = select(slot_rows(ahead[...], 1, most), source[...])


def relay_kernel(crossed, target, after, out_here, out_there):
    del after
    most = out_here.shape[0]
    out_here[...] = select(slot_rows(target[...], 2, most), crossed[...])
    out_there[...] = select(slot_rows(target[...], 3, most), crossed[...])


def own_kernel(
    own, target, chosen, mod, router, w1, w2, after, out, gates, w1v, w2v, x, hidden, sems1, sems2
):
    del after

    def copies(source, target, sems):
        return [
            pltpu.make_async_copy(
                source.at[:, pl.ds(start, size)], target.at[:, pl.ds(start, size)], sems.at[index]
            )
            for index, (start, size) in enumerate(tiles(source.shape[1], 512))
        ]

    first, second = copies(w1, w1v, sems1), copies(w2, w2v, sems2)
    for copy in first + second:
        copy.start()
    most = out.shape[0]
    modulated = modulate(own[...], mod[0:1, :], mod[1:2, :])
    logits = lax.dot_general(
        router[...], modulated, (((1,), (1,)), ((), ())), preferred_element_type=jnp.float32
    )
    picked = jnp.zeros(chosen.shape, jnp.float32)
    for expert in range(router.shape[0]):
        picked += jnp.where(chosen[...] == expert, logits[expert:expert + 1, :], 0.0)
    sig = jax.nn.sigmoid(picked)
    gates[...] = sig / jnp.sum(sig, axis=0, keepdims=True)
    x[...] = jnp.zeros_like(x)
    x[0:most, :] = select(slot_rows(target[...], 0, most), modulated)
    first_layer(x, w1v, hidden, lambda index: first[index].wait())
    second_layer(hidden, w2v, (0, w2.shape[1]), (out,), lambda index: second[index].wait())


def far_kernel(near_x, far_x, near_z, far_z, mod, w1, w2, after, out_x, out_z, hidden, raw, x):
    del after
    most, cut = near_x.shape
    pad = x.shape[0] // 2
    x[...] = jnp.zeros_like(x)
    for i, (left, right) in enumerate(((near_x, far_x), (near_z, far_z))):
        raw[:, 0:cut] = left[...].astype(jnp.float32)
        raw[:, cut:] = right[...].astype(jnp.float32)
        x[i * pad:i * pad + most, :] = modulate(raw[...], mod[0:1, :], mod[1:2, :])
    first_layer(x, w1, hidden)
    second_layer(hidden, w2, (cut, w2.shape[1]), (out_x, out_z))


def rest_kernel(hidden, w2, after, out_x, out_z):
    del after
    second_layer(hidden, w2, (0, out_x.shape[1]), (out_x, out_z))


def sibling_kernel(sib, mod, w1, w2, after, out, x, hidden):
    del after
    x[...] = jnp.zeros_like(x)
    x[0:out.shape[0], :] = modulate(sib[...], mod[0:1, :], mod[1:2, :])
    first_layer(x, w1, hidden)
    second_layer(hidden, w2, (0, w2.shape[1]), (out,))


def joint_kernel(target, gates, here, there, out):
    value = mixed(target[...], gates[...], 2, here[...])
    value += mixed(target[...], gates[...], 3, there[...])
    out[...] = value.astype(jnp.bfloat16)


def home_kernel(target, gates, y_own, y_x, y_z, out):
    cut = y_own.shape[1] - y_x.shape[1]
    place, weight = target[...], gates[...]
    own = mixed(place, weight, 0, y_own[...])
    far = mixed(place, weight, 2, y_x[...]) + mixed(place, weight, 3, y_z[...])
    out[:, 0:cut] = own[:, 0:cut]
    out[:, cut:] = own[:, cut:] + far


def near_kernel(target, gates, mixture, y_sib, out):
    out[...] = mixture[...] + mixed(target[...], gates[...], 1, y_sib[...])


def last_kernel(incoming, mod, mixture, joint, out):
    cut = joint.shape[1]
    left = mixture[:, 0:cut] + joint[...].astype(jnp.float32)
    left = incoming[:, 0:cut].astype(jnp.float32) + (1.0 + mod[2:3, 0:cut]) * left
    right = incoming[:, cut:].astype(jnp.float32) + (1.0 + mod[2:3, cut:]) * mixture[:, cut:]
    out[:, 0:cut] = left.astype(jnp.bfloat16)
    out[:, cut:] = right.astype(jnp.bfloat16)


def cost(flops):
    return pl.CostEstimate(flops=flops, bytes_accessed=flops // 1024, transcendentals=0)


SHORT, LONG = cost(1 << 20), cost(1 << 37)


def padded(most):
    return -(-most // 16) * 16


def array(rows, columns, dtype=jnp.bfloat16):
    return jax.ShapeDtypeStruct((rows, columns), dtype)


def source_pass(source, ahead, most, cut):
    width = source.shape[1]
    return pl.pallas_call(
        source_kernel,
        out_shape=(array(most, width - cut), array(most, width - cut), array(most, width)),
        in_specs=[VMEM] * 2,
        out_specs=(VMEM,) * 3,
        compiler_params=PARAMS,
        cost_estimate=SHORT,
    )(source, ahead)


def relay_pass(crossed, target, after, most):
    cut = crossed.shape[1]
    return pl.pallas_call(
        relay_kernel,
        out_shape=(array(most, cut), array(most, cut)),
        in_specs=[VMEM] * 2 + [ANY],
        out_specs=(VMEM,) * 2,
        compiler_params=PARAMS,
        cost_estimate=SHORT,
    )(crossed, target, after)


def own_pass(own, target, chosen, mod, router, w1, w2, after, most):
    width, hid = w1.shape
    return pl.pallas_call(
        own_kernel,
        out_shape=(
            array(most, width),
            array(*chosen.shape, jnp.float32),
            pltpu.VMEM(w1.shape, w1.dtype),
            pltpu.VMEM(w2.shape, w2.dtype),
        ),
        in_specs=[VMEM] * 5 + [HBM] * 2 + [ANY],
        out_specs=(VMEM,) * 4,
        scratch_shapes=[
            pltpu.VMEM((padded(most), width), jnp.bfloat16),
            pltpu.VMEM((padded(most), hid), jnp.bfloat16),
            pltpu.SemaphoreType.DMA((len(tiles(w1.shape[1], 512)),)),
            pltpu.SemaphoreType.DMA((len(tiles(w2.shape[1], 512)),)),
        ],
        compiler_params=PARAMS,
        cost_estimate=SHORT,
    )(
        own,
        target,
        chosen,
        mod,
        router,
        pltpu.with_memory_space_constraint(w1, pltpu.HBM),
        pltpu.with_memory_space_constraint(w2, pltpu.HBM),
        after,
    )


def far_pass(near_x, far_x, near_z, far_z, mod, w1, w2, after):
    most = near_x.shape[0]
    width, hid = w1.shape
    out = array(*far_x.shape)
    return pl.pallas_call(
        far_kernel,
        out_shape=(out, out, array(2 * padded(most), hid)),
        in_specs=[VMEM] * 7 + [ANY],
        out_specs=(VMEM,) * 3,
        scratch_shapes=[
            pltpu.VMEM((most, width), jnp.float32),
            pltpu.VMEM((2 * padded(most), width), jnp.bfloat16),
        ],
        compiler_params=PARAMS,
        cost_estimate=SHORT,
    )(near_x, far_x, near_z, far_z, mod, w1, w2, after)


def rest_pass(hidden, w2, after, most, cut):
    return pl.pallas_call(
        rest_kernel,
        out_shape=(array(most, cut), array(most, cut)),
        in_specs=[VMEM] * 2 + [ANY],
        out_specs=(VMEM,) * 2,
        compiler_params=PARAMS,
        cost_estimate=SHORT,
    )(hidden, w2, after)


def sibling_pass(sib, mod, w1, w2, after):
    most, width = sib.shape
    hid = w1.shape[1]
    return pl.pallas_call(
        sibling_kernel,
        out_shape=array(most, width),
        in_specs=[VMEM] * 4 + [ANY],
        out_specs=VMEM,
        scratch_shapes=[
            pltpu.VMEM((padded(most), width), jnp.bfloat16),
            pltpu.VMEM((padded(most), hid), jnp.bfloat16),
        ],
        compiler_params=PARAMS,
        cost_estimate=SHORT,
    )(sib, mod, w1, w2, after)


def joint_pass(target, gates, here, there):
    tokens, cut = target.shape[1], here.shape[1]
    return pl.pallas_call(
        joint_kernel,
        out_shape=array(tokens, cut),
        in_specs=[VMEM] * 4,
        out_specs=VMEM,
        compiler_params=PARAMS,
        cost_estimate=SHORT,
    )(target, gates, here, there)


def home_pass(target, gates, y_own, y_x, y_z):
    return pl.pallas_call(
        home_kernel,
        out_shape=array(target.shape[1], y_own.shape[1], jnp.float32),
        in_specs=[VMEM] * 5,
        out_specs=VMEM,
        compiler_params=PARAMS,
        cost_estimate=LONG,
    )(target, gates, y_own, y_x, y_z)


def near_pass(target, gates, mixture, y_sib):
    return pl.pallas_call(
        near_kernel,
        out_shape=array(*mixture.shape, jnp.float32),
        in_specs=[VMEM] * 4,
        out_specs=VMEM,
        compiler_params=PARAMS,
        cost_estimate=SHORT,
    )(target, gates, mixture, y_sib)


def last_pass(incoming, mod, mixture, joint):
    return pl.pallas_call(
        last_kernel,
        out_shape=array(*incoming.shape),
        in_specs=[VMEM] * 4,
        out_specs=VMEM,
        compiler_params=PARAMS,
        cost_estimate=SHORT,
    )(incoming, mod, mixture, joint)


def quad_body(states, routes, slots, timesteps, router_weight, expert_in, expert_out, modulation):
    source = states[0]
    width = source.shape[1]
    most = 3 * source.shape[0] // 4
    cut = width // 256 * 128
    here = lax.axis_index("expert")
    chosen = routes[0].T
    target = (chosen ^ here) * most + slots[0].T
    x_target = swapped(target, 2)
    ahead = shifted(target, "comp", -1)
    crossed = advanced(source[:, :cut], 2)
    incoming = shifted(source, "comp", 1)
    mod = modulation[timesteps[0]].astype(jnp.float32)

    x_source, z_source, s_source = source_pass(source, ahead, most, cut)
    sib = advanced(s_source, 1)
    far_x = advanced(x_source, 2)
    far_z = advanced(z_source, 3)

    y_own, gates, w1, w2 = own_pass(
        incoming,
        target,
        chosen,
        mod,
        router_weight[0].T,
        expert_in[0],
        expert_out[0],
        z_source,
        most,
    )
    x_gates = swapped(gates, 2)
    w1 = pltpu.with_memory_space_constraint(w1, pltpu.VMEM)
    w2 = pltpu.with_memory_space_constraint(w2, pltpu.VMEM)
    near_x, passed = relay_pass(crossed, x_target, gates, most)
    near_z = swapped(passed, 1)
    y_sib = sibling_pass(sib, mod, w1, w2, passed)
    back_s = swapped(y_sib, 1)
    x_right, z_right, hidden = far_pass(
        near_x, far_x, near_z, far_z, mod, w1, w2, y_sib
    )
    back_z = swapped(z_right, 3)
    back_x = swapped(x_right, 2)
    x_left, z_left = rest_pass(hidden, w2, x_gates, most, cut)
    lent = swapped(z_left, 1)
    joint = swapped(joint_pass(x_target, x_gates, x_left, lent), 2)
    mixture = home_pass(target, gates, y_own, back_x, back_z)
    mixture = near_pass(target, gates, mixture, back_s)
    return last_pass(incoming, mod, mixture, joint)[None]


def gating(modulated, weight, chosen):
    logits = jnp.dot(modulated, weight, preferred_element_type=jnp.float32)
    picks = chosen[..., None] == jnp.arange(weight.shape[1], dtype=jnp.int32)
    selected = jnp.sum(jnp.where(picks, logits[:, None, :], jnp.float32(0.0)), axis=-1)
    sig = jax.nn.sigmoid(selected)
    return sig / jnp.sum(sig, axis=1, keepdims=True)


def general_body(states, routes, slots, timesteps, router_weight, expert_in, expert_out, modulation):
    devices = lax.axis_size("expert")
    tokens_here = states.shape[1]
    width = states.shape[2]
    experts = router_weight.shape[2]
    shards = devices // experts
    most = 3 * tokens_here // 4
    incoming = shifted(states[0], "comp", 1)
    mod = modulation[timesteps[0]].astype(jnp.float32)
    modulated = modulate(incoming, mod[0], mod[1])
    chosen = routes[0]
    gates = gating(modulated, router_weight[0], chosen)
    target = chosen * most + slots[0]
    place = target[..., None] == jnp.arange(experts * most, dtype=jnp.int32)
    occupied = jnp.any(place, axis=1).astype(jnp.bfloat16)
    buffer = jnp.einsum(
        "tr,td->rd", occupied, modulated, preferred_element_type=jnp.float32
    ).astype(jnp.bfloat16)
    mix_weights = jnp.sum(jnp.where(place, gates[..., None], jnp.float32(0.0)), axis=1)
    w_first = expert_in[0]
    w_second = expert_out[0]
    copies = jnp.broadcast_to(
        buffer.reshape(experts, 1, most, width), (experts, shards, most, width)
    )
    outgoing = copies.reshape(devices, most, width)
    received = lax.all_to_all(outgoing, "expert", split_axis=0, concat_axis=0, tiled=True)
    count = received.shape[1]
    hidden = jax.nn.gelu(
        jnp.dot(received.reshape(-1, width), w_first, preferred_element_type=jnp.float32),
        approximate=True,
    )
    partial_value = (
        jnp.dot(hidden.astype(jnp.bfloat16), w_second, preferred_element_type=jnp.float32)
        .astype(jnp.bfloat16)
        .reshape(devices, count, width)
    )
    returned = lax.all_to_all(partial_value, "expert", split_axis=0, concat_axis=0, tiled=True)
    combined = jnp.sum(returned.reshape(experts, shards, most, width).astype(jnp.float32), axis=1)
    mixture = jnp.dot(
        mix_weights,
        combined.reshape(experts * most, width),
        precision=lax.Precision.HIGHEST,
        preferred_element_type=jnp.float32,
    )
    updated = incoming.astype(jnp.float32) + (1.0 + mod[2]) * mixture
    return updated.astype(jnp.bfloat16)[None]


def body(states, routes, slots, timesteps, router_weight, *rest):
    quad = lax.axis_size("expert") == router_weight.shape[2] == 4
    chosen_body = quad_body if quad else general_body
    return chosen_body(states, routes, slots, timesteps, router_weight, *rest)


def solution(mesh):
    in_specs = (
        P("comp", ("groups", "expert"), None),
        P("comp", ("groups", "expert"), None),
        P("comp", ("groups", "expert"), None),
        P(("groups", "comp")),
        P("comp", None, None),
        P("comp", None, "expert"),
        P("comp", "expert", None),
        P(),
    )
    out_specs = P("comp", ("groups", "expert"), None)
    return jax.shard_map(body, mesh=mesh, in_specs=in_specs, out_specs=out_specs, check_vma=False)
```

```python
import functools

import jax
import jax.numpy as jnp
from jax import lax
from jax.experimental import pallas as pl
from jax.experimental.pallas import tpu as pltpu
from jax.sharding import PartitionSpec as P

MIB = 1024 * 1024
VMEM = pl.BlockSpec(memory_space=pltpu.VMEM)
ANY = pl.BlockSpec(memory_space=pl.ANY)
HBM = pl.BlockSpec(memory_space=pltpu.HBM)
PARAMS = pltpu.CompilerParams(vmem_limit_bytes=10 * MIB)


def shifted(block, axis, distance):
    devices = range(lax.axis_size(axis))
    route = [((i - distance) % len(devices), i) for i in devices]
    return lax.ppermute(block, axis, route)


def swapped(block, mask):
    return lax.ppermute(block, "expert", [(e, e ^ mask) for e in range(lax.axis_size("expert"))])


def advanced(block, mask):
    comps, experts = lax.axis_size("comp"), lax.axis_size("expert")
    route = [
        (c * experts + e, (c + 1) % comps * experts + (e ^ mask))
        for c in range(comps)
        for e in range(experts)
    ]
    return lax.ppermute(block, ("comp", "expert"), route)


def modulate(incoming, scale, shift):
    values = incoming.astype(jnp.float32)
    centred = values - jnp.mean(values, axis=-1, keepdims=True)
    spread = jnp.mean(centred * centred, axis=-1, keepdims=True)
    normed = centred * lax.rsqrt(spread + 1e-06)
    return (normed * (1.0 + scale) + shift).astype(jnp.bfloat16)


def slot_rows(target, mask, most):
    rows = lax.broadcasted_iota(jnp.int32, (most, target.shape[1]), 0) + mask * most
    hit = (rows == target[0:1, :]) | (rows == target[1:2, :])
    return jnp.where(hit, 1.0, 0.0).astype(jnp.bfloat16)


def select(rows, block):
    return jnp.dot(rows, block, preferred_element_type=jnp.float32).astype(jnp.bfloat16)


def gate_column(target, gates, mask, most):
    picked = (target >= mask * most) & (target < (mask + 1) * most)
    row = jnp.sum(jnp.where(picked, gates, 0.0), axis=0, keepdims=True)
    size = target.shape[1]
    places = (size, size)
    same = lax.broadcasted_iota(jnp.int32, places, 0) == lax.broadcasted_iota(jnp.int32, places, 1)
    return jnp.sum(jnp.where(same, row, 0.0), axis=1, keepdims=True)


def mixed(target, gates, mask, result):
    rows = slot_rows(target, mask, result.shape[0])
    spread = lax.dot_general(
        rows, result, (((0,), (0,)), ((), ())), preferred_element_type=jnp.float32
    )
    return gate_column(target, gates, mask, result.shape[0]) * spread


def tiles(size, step):
    return [(i, min(step, size - i)) for i in range(0, size, step)]


def first_layer(x, w1, hidden, ready=lambda index: None):
    for index, (start, size) in enumerate(tiles(w1.shape[1], 512)):
        ready(index)
        value = jnp.dot(x[...], w1[:, start:start + size], preferred_element_type=jnp.float32)
        hidden[:, start:start + size] = jax.nn.gelu(value, approximate=True).astype(jnp.bfloat16)


def second_layer(hidden, w2, columns, outs, ready=lambda index: None):
    pad = hidden.shape[0] // len(outs)
    for index, (start, size) in enumerate(tiles(columns[1] - columns[0], 512)):
        ready(index)
        part = w2[:, columns[0] + start:columns[0] + start + size]
        value = jnp.dot(hidden[...], part, preferred_element_type=jnp.float32)
        for i, out in enumerate(outs):
            rows = value[i * pad:i * pad + out.shape[0]]
            out[:, start:start + size] = rows.astype(jnp.bfloat16)


def sibling_kernel(source, ahead, out, out_source):
    out[...] = select(slot_rows(ahead[...], 1, out.shape[0]), source[...])
    out_source[...] = source[...]


def source_kernel(mask, source, ahead, after, out):
    del after
    first = source.shape[1] - out.shape[1]
    out[...] = select(slot_rows(ahead[...], mask, out.shape[0]), source[:, first:])


def load_kernel(weight, after, out, sems):
    del after
    copies = [
        pltpu.make_async_copy(
            weight.at[:, pl.ds(start, size)], out.at[:, pl.ds(start, size)], sems.at[index]
        )
        for index, (start, size) in enumerate(tiles(weight.shape[1], 512))
    ]
    for copy in copies:
        copy.start()
    for copy in copies:
        copy.wait()


def relay_kernel(crossed, target, after, out_here, out_there):
    del after
    most = out_here.shape[0]
    out_here[...] = select(slot_rows(target[...], 2, most), crossed[...])
    out_there[...] = select(slot_rows(target[...], 3, most), crossed[...])


def gate_kernel(own, target, chosen, mod, router, out, gates):
    modulated = modulate(own[...], mod[0:1, :], mod[1:2, :])
    logits = lax.dot_general(
        router[...], modulated, (((1,), (1,)), ((), ())), preferred_element_type=jnp.float32
    )
    picked = jnp.zeros(chosen.shape, jnp.float32)
    for expert in range(router.shape[0]):
        picked += jnp.where(chosen[...] == expert, logits[expert:expert + 1, :], 0.0)
    sig = jax.nn.sigmoid(picked)
    gates[...] = sig / jnp.sum(sig, axis=0, keepdims=True)
    out[...] = select(slot_rows(target[...], 0, out.shape[0]), modulated)


def pack_gates(gates, rows):
    row = lax.broadcasted_iota(jnp.int32, (rows, gates.shape[1]), 0)
    packed = jnp.zeros(row.shape, jnp.float32)
    for index in range(3):
        piece = gates.astype(jnp.bfloat16).astype(jnp.float32)
        gates = gates - piece
        for k in range(2):
            packed = jnp.where(row == 2 * index + k, piece[k:k + 1, :], packed)
    return packed.astype(jnp.bfloat16)


def unpack_gates(packed):
    pieces = packed[0:16, :].astype(jnp.float32)
    return (pieces[0:2, :] + pieces[2:4, :]) + pieces[4:6, :]


def far_hidden(left, right, mod, w1, hidden, raw, x):
    most, cut = left.shape
    raw[:, 0:cut] = left[...].astype(jnp.float32)
    raw[:, cut:] = right[...].astype(jnp.float32)
    for start, size in tiles(most, 16):
        x[start:start + size, :] = modulate(raw[start:start + size, :], mod[0:1, :], mod[1:2, :])
    first_layer(x, w1, hidden)


def cross_kernel(left, right, mod, gates, w1, w2, out, hidden, raw, x):
    width = w2.shape[1]
    part = out.shape[1] - gates.shape[1]
    out[:, part:] = pack_gates(gates[...], out.shape[0])
    far_hidden(left, right, mod, w1, hidden, raw, x)
    second_layer(hidden, w2, (width - part, width), (out.at[:, 0:part],))


def far_kernel(left, right, mod, w1, w2, after, out_left, out_right, hidden, raw, x):
    del after
    cut = out_left.shape[1]
    far_hidden(left, right, mod, w1, hidden, raw, x)
    second_layer(hidden, w2, (0, cut), (out_left,))
    second_layer(hidden, w2, (cut, w2.shape[1]), (out_right,))


def rest_kernel(hidden, w2, after, out):
    del after
    second_layer(hidden, w2, (0, out.shape[1]), (out,))


def near_kernel(own, sib, mod, w1, w2, after, out_own, out_first, out_second, x, hidden):
    del after
    most, pad = own.shape[0], x.shape[0] // 2
    x[...] = jnp.zeros_like(x)
    x[0:most, :] = own[...]
    x[pad:pad + most, :] = modulate(sib[...], mod[0:1, :], mod[1:2, :])
    first_layer(x, w1, hidden)
    cut = out_first.shape[1]
    second_layer(hidden, w2, (0, cut), (out_own.at[:, 0:cut], out_first))
    second_layer(hidden, w2, (cut, w2.shape[1]), (out_own.at[:, cut:], out_second))


def joint_kernel(target, carried, here, there, later, after, out, out_later):
    del after
    out_later[...] = later[...]
    gates = unpack_gates(carried[:, carried.shape[1] - target.shape[1]:])
    value = mixed(target[...], gates, 2, here[...])
    value += mixed(target[...], gates, 3, there[...])
    out[...] = value.astype(jnp.bfloat16)


def home_kernel(target, gates, y_own, y_x, y_z, out):
    part = y_z.shape[1]
    cut = y_own.shape[1] - part
    place, weight = target[...], gates[...]
    own = mixed(place, weight, 0, y_own[...])
    far = mixed(place, weight, 2, y_x[:, 0:part]) + mixed(place, weight, 3, y_z[...])
    out[:, 0:cut] = own[:, 0:cut]
    out[:, cut:] = own[:, cut:] + far


def add_kernel(target, gates, mixture, y_first, y_second, out):
    cut = y_first.shape[1]
    place, weight = target[...], gates[...]
    out[:, 0:cut] = mixture[:, 0:cut] + mixed(place, weight, 1, y_first[...])
    out[:, cut:] = mixture[:, cut:] + mixed(place, weight, 1, y_second[...])


def last_kernel(incoming, mod, mixture, joint, out):
    cut = joint.shape[1]
    left = mixture[:, 0:cut] + joint[...].astype(jnp.float32)
    left = incoming[:, 0:cut].astype(jnp.float32) + (1.0 + mod[2:3, 0:cut]) * left
    right = incoming[:, cut:].astype(jnp.float32) + (1.0 + mod[2:3, cut:]) * mixture[:, cut:]
    out[:, 0:cut] = left.astype(jnp.bfloat16)
    out[:, cut:] = right.astype(jnp.bfloat16)


def cost(flops):
    return pl.CostEstimate(flops=flops, bytes_accessed=flops // 1024, transcendentals=0)


SHORT, LONG = cost(1 << 20), cost(1 << 37)


def padded(most):
    return -(-most // 16) * 16


def array(rows, columns, dtype=jnp.bfloat16):
    return jax.ShapeDtypeStruct((rows, columns), dtype)


def sibling_pass(source, ahead, most):
    return pl.pallas_call(
        sibling_kernel,
        out_shape=(array(most, source.shape[1]), array(*source.shape)),
        in_specs=[VMEM] * 2,
        out_specs=(VMEM,) * 2,
        compiler_params=PARAMS,
        cost_estimate=SHORT,
    )(source, ahead)


def source_pass(mask, source, ahead, after, most, first):
    return pl.pallas_call(
        functools.partial(source_kernel, mask),
        out_shape=array(most, source.shape[1] - first),
        in_specs=[VMEM] * 2 + [ANY],
        out_specs=VMEM,
        compiler_params=PARAMS,
        cost_estimate=SHORT,
    )(source, ahead, after)


def load_pass(weight, after):
    loaded = pl.pallas_call(
        load_kernel,
        out_shape=pltpu.VMEM(weight.shape, weight.dtype),
        in_specs=[HBM, ANY],
        out_specs=VMEM,
        scratch_shapes=[pltpu.SemaphoreType.DMA((len(tiles(weight.shape[1], 512)),))],
        compiler_params=PARAMS,
        cost_estimate=SHORT,
    )(pltpu.with_memory_space_constraint(weight, pltpu.HBM), after)
    return pltpu.with_memory_space_constraint(loaded, pltpu.VMEM)


def relay_pass(crossed, target, after, most):
    part = array(most, crossed.shape[1])
    return pl.pallas_call(
        relay_kernel,
        out_shape=(part, part),
        in_specs=[VMEM] * 2 + [ANY],
        out_specs=(VMEM,) * 2,
        compiler_params=PARAMS,
        cost_estimate=SHORT,
    )(crossed, target, after)


def gate_pass(own, target, chosen, mod, router, most):
    return pl.pallas_call(
        gate_kernel,
        out_shape=(array(most, own.shape[1]), array(*chosen.shape, jnp.float32)),
        in_specs=[VMEM] * 5,
        out_specs=(VMEM,) * 2,
        compiler_params=PARAMS,
        cost_estimate=SHORT,
    )(own, target, chosen, mod, router)


def cross_pass(left, right, mod, gates, w1, w2, cut):
    most = left.shape[0]
    width, hid = w1.shape
    return pl.pallas_call(
        cross_kernel,
        out_shape=(array(most, width - cut + gates.shape[1]), array(most, hid)),
        in_specs=[VMEM] * 6,
        out_specs=(VMEM,) * 2,
        scratch_shapes=[
            pltpu.VMEM((most, width), jnp.float32),
            pltpu.VMEM((most, width), jnp.bfloat16),
        ],
        compiler_params=PARAMS,
        cost_estimate=SHORT,
    )(left, right, mod, gates, w1, w2)


def far_pass(left, right, mod, w1, w2, after, cut):
    most = left.shape[0]
    width, hid = w1.shape
    return pl.pallas_call(
        far_kernel,
        out_shape=(array(most, cut), array(most, width - cut)),
        in_specs=[VMEM] * 5 + [ANY],
        out_specs=(VMEM,) * 2,
        scratch_shapes=[
            pltpu.VMEM((most, hid), jnp.bfloat16),
            pltpu.VMEM((most, width), jnp.float32),
            pltpu.VMEM((most, width), jnp.bfloat16),
        ],
        compiler_params=PARAMS,
        cost_estimate=SHORT,
    )(left, right, mod, w1, w2, after)


def rest_pass(hidden, w2, after, cut):
    return pl.pallas_call(
        rest_kernel,
        out_shape=array(hidden.shape[0], cut),
        in_specs=[VMEM] * 2 + [ANY],
        out_specs=VMEM,
        compiler_params=PARAMS,
        cost_estimate=SHORT,
    )(hidden, w2, after)


def near_pass(own, sib, mod, w1, w2, after, cut):
    most, width = sib.shape
    return pl.pallas_call(
        near_kernel,
        out_shape=(array(most, width), array(most, cut), array(most, width - cut)),
        in_specs=[VMEM] * 5 + [ANY],
        out_specs=(VMEM,) * 3,
        scratch_shapes=[
            pltpu.VMEM((2 * padded(most), width), jnp.bfloat16),
            pltpu.VMEM((2 * padded(most), w1.shape[1]), jnp.bfloat16),
        ],
        compiler_params=PARAMS,
        cost_estimate=SHORT,
    )(own, sib, mod, w1, w2, after)


def joint_pass(target, carried, here, there, later, after):
    return pl.pallas_call(
        joint_kernel,
        out_shape=(array(target.shape[1], here.shape[1]), array(*later.shape)),
        in_specs=[VMEM] * 5 + [ANY],
        out_specs=(VMEM,) * 2,
        compiler_params=PARAMS,
        cost_estimate=SHORT,
    )(target, carried, here, there, later, after)


def home_pass(target, gates, y_own, y_x, y_z):
    return pl.pallas_call(
        home_kernel,
        out_shape=array(target.shape[1], y_own.shape[1], jnp.float32),
        in_specs=[VMEM] * 5,
        out_specs=VMEM,
        compiler_params=PARAMS,
        cost_estimate=LONG,
    )(target, gates, y_own, y_x, y_z)


def add_pass(target, gates, mixture, y_first, y_second):
    return pl.pallas_call(
        add_kernel,
        out_shape=array(*mixture.shape, jnp.float32),
        in_specs=[VMEM] * 5,
        out_specs=VMEM,
        compiler_params=PARAMS,
        cost_estimate=SHORT,
    )(target, gates, mixture, y_first, y_second)


def last_pass(incoming, mod, mixture, joint):
    return pl.pallas_call(
        last_kernel,
        out_shape=array(*incoming.shape),
        in_specs=[VMEM] * 4,
        out_specs=VMEM,
        compiler_params=PARAMS,
        cost_estimate=SHORT,
    )(incoming, mod, mixture, joint)


def quad_body(states, routes, slots, timesteps, router_weight, expert_in, expert_out, modulation):
    source = states[0]
    width = source.shape[1]
    most = 3 * source.shape[0] // 4
    cut = width // 256 * 128
    back_cut = cut
    here = lax.axis_index("expert")
    chosen = routes[0].T
    target = (chosen ^ here) * most + slots[0].T
    x_target = swapped(target, 2)
    ahead = shifted(target, "comp", -1)
    crossed = advanced(source[:, :cut], 2)
    mod = modulation[timesteps[0]].astype(jnp.float32)

    s_source, same = sibling_pass(source, ahead, most)
    incoming = shifted(same, "comp", 1)
    sib = advanced(s_source, 1)
    w1 = load_pass(expert_in[0], s_source)
    far_x = advanced(source_pass(2, source, ahead, w1, most, cut), 2)
    own, gates = gate_pass(incoming, target, chosen, mod, router_weight[0].T, most)

    near_x, passed = relay_pass(crossed, x_target, w1, most)
    near_z = swapped(passed, 1)
    z_source = source_pass(3, source, ahead, passed, most, cut)
    far_z = advanced(z_source, 3)
    w2 = load_pass(expert_out[0], z_source)
    x_right, x_hidden = cross_pass(near_x, far_x, mod, gates, w1, w2, back_cut)
    back_x = swapped(x_right, 2)
    y_own, s_first, s_second = near_pass(own, sib, mod, w1, w2, x_right, cut + 256)
    back_first = swapped(s_first, 1)
    z_left, z_right = far_pass(near_z, far_z, mod, w1, w2, s_first, back_cut)
    lent = swapped(z_left, 1)
    back_z = swapped(z_right, 3)
    x_left = rest_pass(x_hidden, w2, z_left, back_cut)
    joint, later = joint_pass(x_target, back_x, x_left, lent, s_second, back_first)
    joint = swapped(joint, 2)
    back_second = swapped(later, 1)
    mixture = home_pass(target, gates, y_own, back_x, back_z)
    mixture = add_pass(target, gates, mixture, back_first, back_second)
    return last_pass(incoming, mod, mixture, joint)[None]


def gating(modulated, weight, chosen):
    logits = jnp.dot(modulated, weight, preferred_element_type=jnp.float32)
    picks = chosen[..., None] == jnp.arange(weight.shape[1], dtype=jnp.int32)
    selected = jnp.sum(jnp.where(picks, logits[:, None, :], jnp.float32(0.0)), axis=-1)
    sig = jax.nn.sigmoid(selected)
    return sig / jnp.sum(sig, axis=1, keepdims=True)


def general_body(states, routes, slots, timesteps, router_weight, expert_in, expert_out, modulation):
    devices = lax.axis_size("expert")
    tokens_here = states.shape[1]
    width = states.shape[2]
    experts = router_weight.shape[2]
    shards = devices // experts
    most = 3 * tokens_here // 4
    incoming = shifted(states[0], "comp", 1)
    mod = modulation[timesteps[0]].astype(jnp.float32)
    modulated = modulate(incoming, mod[0], mod[1])
    chosen = routes[0]
    gates = gating(modulated, router_weight[0], chosen)
    target = chosen * most + slots[0]
    place = target[..., None] == jnp.arange(experts * most, dtype=jnp.int32)
    occupied = jnp.any(place, axis=1).astype(jnp.bfloat16)
    buffer = jnp.einsum(
        "tr,td->rd", occupied, modulated, preferred_element_type=jnp.float32
    ).astype(jnp.bfloat16)
    mix_weights = jnp.sum(jnp.where(place, gates[..., None], jnp.float32(0.0)), axis=1)
    w_first = expert_in[0]
    w_second = expert_out[0]
    copies = jnp.broadcast_to(
        buffer.reshape(experts, 1, most, width), (experts, shards, most, width)
    )
    outgoing = copies.reshape(devices, most, width)
    received = lax.all_to_all(outgoing, "expert", split_axis=0, concat_axis=0, tiled=True)
    count = received.shape[1]
    hidden = jax.nn.gelu(
        jnp.dot(received.reshape(-1, width), w_first, preferred_element_type=jnp.float32),
        approximate=True,
    )
    partial_value = (
        jnp.dot(hidden.astype(jnp.bfloat16), w_second, preferred_element_type=jnp.float32)
        .astype(jnp.bfloat16)
        .reshape(devices, count, width)
    )
    returned = lax.all_to_all(partial_value, "expert", split_axis=0, concat_axis=0, tiled=True)
    combined = jnp.sum(returned.reshape(experts, shards, most, width).astype(jnp.float32), axis=1)
    mixture = jnp.dot(
        mix_weights,
        combined.reshape(experts * most, width),
        precision=lax.Precision.HIGHEST,
        preferred_element_type=jnp.float32,
    )
    updated = incoming.astype(jnp.float32) + (1.0 + mod[2]) * mixture
    return updated.astype(jnp.bfloat16)[None]


def body(states, routes, slots, timesteps, router_weight, *rest):
    quad = lax.axis_size("expert") == router_weight.shape[2] == 4
    chosen_body = quad_body if quad else general_body
    return chosen_body(states, routes, slots, timesteps, router_weight, *rest)


def solution(mesh):
    in_specs = (
        P("comp", ("groups", "expert"), None),
        P("comp", ("groups", "expert"), None),
        P("comp", ("groups", "expert"), None),
        P(("groups", "comp")),
        P("comp", None, None),
        P("comp", None, "expert"),
        P("comp", "expert", None),
        P(),
    )
    out_specs = P("comp", ("groups", "expert"), None)
    return jax.shard_map(body, mesh=mesh, in_specs=in_specs, out_specs=out_specs, check_vma=False)
```

```python
import functools

import jax
import jax.numpy as jnp
from jax import lax
from jax.experimental import pallas as pl
from jax.experimental.pallas import tpu as pltpu
from jax.sharding import PartitionSpec as P

MIB = 1024 * 1024
VMEM = pl.BlockSpec(memory_space=pltpu.VMEM)
ANY = pl.BlockSpec(memory_space=pl.ANY)
HBM = pl.BlockSpec(memory_space=pltpu.HBM)
PARAMS = pltpu.CompilerParams(vmem_limit_bytes=10 * MIB)


def shifted(block, axis, distance):
    devices = range(lax.axis_size(axis))
    route = [((i - distance) % len(devices), i) for i in devices]
    return lax.ppermute(block, axis, route)


def swapped(block, mask):
    return lax.ppermute(block, "expert", [(e, e ^ mask) for e in range(lax.axis_size("expert"))])


def advanced(block, mask):
    comps, experts = lax.axis_size("comp"), lax.axis_size("expert")
    route = [
        (c * experts + e, (c + 1) % comps * experts + (e ^ mask))
        for c in range(comps)
        for e in range(experts)
    ]
    return lax.ppermute(block, ("comp", "expert"), route)


def modulate(incoming, scale, shift):
    values = incoming.astype(jnp.float32)
    centred = values - jnp.mean(values, axis=-1, keepdims=True)
    spread = jnp.mean(centred * centred, axis=-1, keepdims=True)
    normed = centred * lax.rsqrt(spread + 1e-06)
    return (normed * (1.0 + scale) + shift).astype(jnp.bfloat16)


def slot_rows(target, mask, most):
    rows = lax.broadcasted_iota(jnp.int32, (most, target.shape[1]), 0) + mask * most
    hit = (rows == target[0:1, :]) | (rows == target[1:2, :])
    return jnp.where(hit, 1.0, 0.0).astype(jnp.bfloat16)


def select(rows, block):
    return jnp.dot(rows, block, preferred_element_type=jnp.float32).astype(jnp.bfloat16)


def gate_column(target, gates, mask, most):
    picked = (target >= mask * most) & (target < (mask + 1) * most)
    row = jnp.sum(jnp.where(picked, gates, 0.0), axis=0, keepdims=True)
    size = target.shape[1]
    places = (size, size)
    same = lax.broadcasted_iota(jnp.int32, places, 0) == lax.broadcasted_iota(jnp.int32, places, 1)
    return jnp.sum(jnp.where(same, row, 0.0), axis=1, keepdims=True)


def mixed(target, gates, mask, result):
    rows = slot_rows(target, mask, result.shape[0])
    spread = lax.dot_general(
        rows, result, (((0,), (0,)), ((), ())), preferred_element_type=jnp.float32
    )
    return gate_column(target, gates, mask, result.shape[0]) * spread


def tiles(size, step):
    return [(i, min(step, size - i)) for i in range(0, size, step)]


def first_layer(x, w1, hidden, ready=lambda index: None):
    for index, (start, size) in enumerate(tiles(w1.shape[1], 512)):
        ready(index)
        value = jnp.dot(x[...], w1[:, start:start + size], preferred_element_type=jnp.float32)
        hidden[:, start:start + size] = jax.nn.gelu(value, approximate=True).astype(jnp.bfloat16)


def second_layer(hidden, w2, columns, outs, ready=lambda index: None):
    pad = hidden.shape[0] // len(outs)
    for index, (start, size) in enumerate(tiles(columns[1] - columns[0], 512)):
        ready(index)
        part = w2[:, columns[0] + start:columns[0] + start + size]
        value = jnp.dot(hidden[...], part, preferred_element_type=jnp.float32)
        for i, out in enumerate(outs):
            rows = value[i * pad:i * pad + out.shape[0]]
            out[:, start:start + size] = rows.astype(jnp.bfloat16)


def sibling_kernel(source, ahead, target, out, out_source, out_target):
    out_target[...] = target[...]
    out[...] = select(slot_rows(ahead[...], 1, out.shape[0]), source[...])
    out_source[...] = source[...]


def source_kernel(mask, source, ahead, after, out):
    del after
    first = source.shape[1] - out.shape[1]
    out[...] = select(slot_rows(ahead[...], mask, out.shape[0]), source[:, first:])


def load_kernel(weight, after, out, sems):
    del after
    copies = [
        pltpu.make_async_copy(
            weight.at[:, pl.ds(start, size)], out.at[:, pl.ds(start, size)], sems.at[index]
        )
        for index, (start, size) in enumerate(tiles(weight.shape[1], 512))
    ]
    for copy in copies:
        copy.start()
    for copy in copies:
        copy.wait()


def relay_kernel(crossed, target, after, out_here, out_there):
    del after
    most = out_here.shape[0]
    out_here[...] = select(slot_rows(target[...], 2, most), crossed[...])
    out_there[...] = select(slot_rows(target[...], 3, most), crossed[...])


def gate_kernel(own, target, chosen, mod, router, out, gates):
    modulated = modulate(own[...], mod[0:1, :], mod[1:2, :])
    logits = lax.dot_general(
        router[...], modulated, (((1,), (1,)), ((), ())), preferred_element_type=jnp.float32
    )
    picked = jnp.zeros(chosen.shape, jnp.float32)
    for expert in range(router.shape[0]):
        picked += jnp.where(chosen[...] == expert, logits[expert:expert + 1, :], 0.0)
    sig = jax.nn.sigmoid(picked)
    gates[...] = sig / jnp.sum(sig, axis=0, keepdims=True)
    out[...] = select(slot_rows(target[...], 0, out.shape[0]), modulated)


def pack_gates(gates, rows):
    row = lax.broadcasted_iota(jnp.int32, (rows, gates.shape[1]), 0)
    packed = jnp.zeros(row.shape, jnp.float32)
    for index in range(3):
        piece = gates.astype(jnp.bfloat16).astype(jnp.float32)
        gates = gates - piece
        for k in range(2):
            packed = jnp.where(row == 2 * index + k, piece[k:k + 1, :], packed)
    return packed.astype(jnp.bfloat16)


def unpack_gates(packed):
    pieces = packed[0:16, :].astype(jnp.float32)
    return (pieces[0:2, :] + pieces[2:4, :]) + pieces[4:6, :]


def far_hidden(left, right, mod, w1, hidden, raw, x):
    most, cut = left.shape
    raw[:, 0:cut] = left[...].astype(jnp.float32)
    raw[:, cut:] = right[...].astype(jnp.float32)
    for start, size in tiles(most, 16):
        x[start:start + size, :] = modulate(raw[start:start + size, :], mod[0:1, :], mod[1:2, :])
    first_layer(x, w1, hidden)


def cross_kernel(left, right, mod, gates, w1, w2, out, hidden, raw, x):
    width = w2.shape[1]
    part = out.shape[1] - gates.shape[1]
    out[:, part:] = pack_gates(gates[...], out.shape[0])
    far_hidden(left, right, mod, w1, hidden, raw, x)
    second_layer(hidden, w2, (width - part, width), (out.at[:, 0:part],))


def far_kernel(
    left, right, mod, w1, w2, x_hidden, after, out_x, out_z, z_hidden, hidden, raw, x
):
    del after
    most, cut = left.shape
    pad = hidden.shape[0] // 2
    hidden[...] = jnp.zeros_like(hidden)
    hidden[0:most, :] = x_hidden[...]
    far_hidden(left, right, mod, w1, hidden.at[pad:pad + most, :], raw, x)
    z_hidden[...] = hidden[pad:pad + most, :]
    second_layer(hidden, w2, (0, out_x.shape[1]), (out_x, out_z))


def rest_kernel(hidden, w2, out):
    second_layer(hidden, w2, (w2.shape[1] - out.shape[1], w2.shape[1]), (out,))


def near_kernel(own, sib, mod, w1, w2, after, out_own, out_first, out_second, raw, x, hidden):
    del after
    most = own.shape[0]
    raw[0:most, :] = own[...].astype(jnp.float32)
    for start, size in tiles(most, 16):
        rows = modulate(sib[start:start + size, :], mod[0:1, :], mod[1:2, :])
        raw[most + start:most + start + size, :] = rows.astype(jnp.float32)
    x[...] = raw[...].astype(jnp.bfloat16)
    first_layer(x, w1, hidden)
    cut = out_first.shape[1]
    second_layer(hidden, w2, (0, cut), (out_own.at[:, 0:cut], out_first))
    second_layer(hidden, w2, (cut, w2.shape[1]), (out_own.at[:, cut:], out_second))


def copy_kernel(source, after, out):
    del after
    out[...] = source[...]


def joint_kernel(target, carried, here, there, after, out):
    del after
    gates = unpack_gates(carried[:, carried.shape[1] - target.shape[1]:])
    value = mixed(target[...], gates, 2, here[...])
    value += mixed(target[...], gates, 3, there[...])
    out[...] = value.astype(jnp.bfloat16)


def home_kernel(target, gates, y_own, y_x, y_z, out):
    part = y_z.shape[1]
    cut = y_own.shape[1] - part
    place, weight = target[...], gates[...]
    own = mixed(place, weight, 0, y_own[...])
    far = mixed(place, weight, 2, y_x[:, 0:part]) + mixed(place, weight, 3, y_z[...])
    out[:, 0:cut] = own[:, 0:cut]
    out[:, cut:] = own[:, cut:] + far


def add_kernel(target, gates, mixture, y_first, y_second, out):
    cut = y_first.shape[1]
    place, weight = target[...], gates[...]
    out[:, 0:cut] = mixture[:, 0:cut] + mixed(place, weight, 1, y_first[...])
    out[:, cut:] = mixture[:, cut:] + mixed(place, weight, 1, y_second[...])


def last_kernel(incoming, mod, mixture, joint, out):
    cut = joint.shape[1]
    left = mixture[:, 0:cut] + joint[...].astype(jnp.float32)
    left = incoming[:, 0:cut].astype(jnp.float32) + (1.0 + mod[2:3, 0:cut]) * left
    right = incoming[:, cut:].astype(jnp.float32) + (1.0 + mod[2:3, cut:]) * mixture[:, cut:]
    out[:, 0:cut] = left.astype(jnp.bfloat16)
    out[:, cut:] = right.astype(jnp.bfloat16)


def cost(flops):
    return pl.CostEstimate(flops=flops, bytes_accessed=flops // 1024, transcendentals=0)


SHORT, LONG = cost(1 << 20), cost(1 << 37)


def padded(most):
    return -(-most // 16) * 16


def array(rows, columns, dtype=jnp.bfloat16):
    return jax.ShapeDtypeStruct((rows, columns), dtype)


def sibling_pass(source, ahead, target, most):
    return pl.pallas_call(
        sibling_kernel,
        out_shape=(
            array(most, source.shape[1]),
            array(*source.shape),
            array(*target.shape, target.dtype),
        ),
        in_specs=[VMEM] * 3,
        out_specs=(VMEM,) * 3,
        compiler_params=PARAMS,
        cost_estimate=SHORT,
    )(source, ahead, target)


def source_pass(mask, source, ahead, after, most, first):
    return pl.pallas_call(
        functools.partial(source_kernel, mask),
        out_shape=array(most, source.shape[1] - first),
        in_specs=[VMEM] * 2 + [ANY],
        out_specs=VMEM,
        compiler_params=PARAMS,
        cost_estimate=SHORT,
    )(source, ahead, after)


def load_pass(weight, after):
    loaded = pl.pallas_call(
        load_kernel,
        out_shape=pltpu.VMEM(weight.shape, weight.dtype),
        in_specs=[HBM, ANY],
        out_specs=VMEM,
        scratch_shapes=[pltpu.SemaphoreType.DMA((len(tiles(weight.shape[1], 512)),))],
        compiler_params=PARAMS,
        cost_estimate=SHORT,
    )(pltpu.with_memory_space_constraint(weight, pltpu.HBM), after)
    return pltpu.with_memory_space_constraint(loaded, pltpu.VMEM)


def relay_pass(crossed, target, after, most):
    part = array(most, crossed.shape[1])
    return pl.pallas_call(
        relay_kernel,
        out_shape=(part, part),
        in_specs=[VMEM] * 2 + [ANY],
        out_specs=(VMEM,) * 2,
        compiler_params=PARAMS,
        cost_estimate=SHORT,
    )(crossed, target, after)


def gate_pass(own, target, chosen, mod, router, most):
    return pl.pallas_call(
        gate_kernel,
        out_shape=(array(most, own.shape[1]), array(*chosen.shape, jnp.float32)),
        in_specs=[VMEM] * 5,
        out_specs=(VMEM,) * 2,
        compiler_params=PARAMS,
        cost_estimate=SHORT,
    )(own, target, chosen, mod, router)


def cross_pass(left, right, mod, gates, w1, w2, cut):
    most = left.shape[0]
    width, hid = w1.shape
    return pl.pallas_call(
        cross_kernel,
        out_shape=(array(most, width - cut + gates.shape[1]), array(most, hid)),
        in_specs=[VMEM] * 6,
        out_specs=(VMEM,) * 2,
        scratch_shapes=[
            pltpu.VMEM((most, width), jnp.float32),
            pltpu.VMEM((most, width), jnp.bfloat16),
        ],
        compiler_params=PARAMS,
        cost_estimate=SHORT,
    )(left, right, mod, gates, w1, w2)


def far_pass(left, right, mod, w1, w2, x_hidden, after, cut):
    most = left.shape[0]
    width, hid = w1.shape
    return pl.pallas_call(
        far_kernel,
        out_shape=(array(most, cut), array(most, cut), array(most, hid)),
        in_specs=[VMEM] * 6 + [ANY],
        out_specs=(VMEM,) * 3,
        scratch_shapes=[
            pltpu.VMEM((2 * padded(most), hid), jnp.bfloat16),
            pltpu.VMEM((most, width), jnp.float32),
            pltpu.VMEM((most, width), jnp.bfloat16),
        ],
        compiler_params=PARAMS,
        cost_estimate=SHORT,
    )(left, right, mod, w1, w2, x_hidden, after)


def rest_pass(hidden, w2, part):
    return pl.pallas_call(
        rest_kernel,
        out_shape=array(hidden.shape[0], part),
        in_specs=[VMEM] * 2,
        out_specs=VMEM,
        compiler_params=PARAMS,
        cost_estimate=SHORT,
    )(hidden, w2)


def near_pass(own, sib, mod, w1, w2, after, cut):
    most, width = sib.shape
    return pl.pallas_call(
        near_kernel,
        out_shape=(array(most, width), array(most, cut), array(most, width - cut)),
        in_specs=[VMEM] * 5 + [ANY],
        out_specs=(VMEM,) * 3,
        scratch_shapes=[
            pltpu.VMEM((2 * most, width), jnp.float32),
            pltpu.VMEM((2 * most, width), jnp.bfloat16),
            pltpu.VMEM((2 * most, w1.shape[1]), jnp.bfloat16),
        ],
        compiler_params=PARAMS,
        cost_estimate=SHORT,
    )(own, sib, mod, w1, w2, after)


def copy_pass(source, after):
    return pl.pallas_call(
        copy_kernel,
        out_shape=array(*source.shape),
        in_specs=[VMEM, ANY],
        out_specs=VMEM,
        compiler_params=PARAMS,
        cost_estimate=SHORT,
    )(source, after)


def joint_pass(target, carried, here, there, after):
    return pl.pallas_call(
        joint_kernel,
        out_shape=array(target.shape[1], here.shape[1]),
        in_specs=[VMEM] * 4 + [ANY],
        out_specs=VMEM,
        compiler_params=PARAMS,
        cost_estimate=SHORT,
    )(target, carried, here, there, after)


def home_pass(target, gates, y_own, y_x, y_z):
    return pl.pallas_call(
        home_kernel,
        out_shape=array(target.shape[1], y_own.shape[1], jnp.float32),
        in_specs=[VMEM] * 5,
        out_specs=VMEM,
        compiler_params=PARAMS,
        cost_estimate=LONG,
    )(target, gates, y_own, y_x, y_z)


def add_pass(target, gates, mixture, y_first, y_second):
    return pl.pallas_call(
        add_kernel,
        out_shape=array(*mixture.shape, jnp.float32),
        in_specs=[VMEM] * 5,
        out_specs=VMEM,
        compiler_params=PARAMS,
        cost_estimate=SHORT,
    )(target, gates, mixture, y_first, y_second)


def last_pass(incoming, mod, mixture, joint):
    return pl.pallas_call(
        last_kernel,
        out_shape=array(*incoming.shape),
        in_specs=[VMEM] * 4,
        out_specs=VMEM,
        compiler_params=PARAMS,
        cost_estimate=SHORT,
    )(incoming, mod, mixture, joint)


def quad_body(states, routes, slots, timesteps, router_weight, expert_in, expert_out, modulation):
    source = states[0]
    width = source.shape[1]
    most = 3 * source.shape[0] // 4
    cut = width // 256 * 128
    back_cut = cut
    sib_cut = cut + 256
    here = lax.axis_index("expert")
    chosen = routes[0].T
    target = (chosen ^ here) * most + slots[0].T
    ahead = shifted(target, "comp", -1)
    crossed = advanced(source[:, :cut], 2)
    mod = modulation[timesteps[0]].astype(jnp.float32)

    s_source, same, same_target = sibling_pass(source, ahead, target, most)
    x_target = swapped(same_target, 2)
    incoming = shifted(same, "comp", 1)
    sib = advanced(s_source, 1)
    w1 = load_pass(expert_in[0], s_source)
    far_x = advanced(source_pass(2, source, ahead, w1, most, cut), 2)
    own, gates = gate_pass(incoming, target, chosen, mod, router_weight[0].T, most)

    near_x, passed = relay_pass(crossed, x_target, w1, most)
    near_z = swapped(passed, 1)
    z_source = source_pass(3, source, ahead, passed, most, cut)
    far_z = advanced(z_source, 3)
    w2 = load_pass(expert_out[0], z_source)
    x_right, x_hidden = cross_pass(near_x, far_x, mod, gates, w1, w2, back_cut)
    back_x = swapped(x_right, 2)
    y_own, s_first, s_second = near_pass(own, sib, mod, w1, w2, x_right, sib_cut)
    back_first = swapped(s_first, 1)
    x_left, z_left, z_hidden = far_pass(
        near_z, far_z, mod, w1, w2, x_hidden, x_hidden, back_cut
    )
    lent = swapped(z_left, 1)
    back_z = swapped(rest_pass(z_hidden, w2, width - back_cut), 3)
    joint = joint_pass(x_target, back_x, x_left, lent, back_first)
    back_second = swapped(copy_pass(s_second, joint), 1)
    joint = swapped(joint, 2)
    mixture = home_pass(target, gates, y_own, back_x, back_z)
    mixture = add_pass(target, gates, mixture, back_first, back_second)
    return last_pass(incoming, mod, mixture, joint)[None]


def gating(modulated, weight, chosen):
    logits = jnp.dot(modulated, weight, preferred_element_type=jnp.float32)
    picks = chosen[..., None] == jnp.arange(weight.shape[1], dtype=jnp.int32)
    selected = jnp.sum(jnp.where(picks, logits[:, None, :], jnp.float32(0.0)), axis=-1)
    sig = jax.nn.sigmoid(selected)
    return sig / jnp.sum(sig, axis=1, keepdims=True)


def general_body(states, routes, slots, timesteps, router_weight, expert_in, expert_out, modulation):
    devices = lax.axis_size("expert")
    tokens_here = states.shape[1]
    width = states.shape[2]
    experts = router_weight.shape[2]
    shards = devices // experts
    most = 3 * tokens_here // 4
    incoming = shifted(states[0], "comp", 1)
    mod = modulation[timesteps[0]].astype(jnp.float32)
    modulated = modulate(incoming, mod[0], mod[1])
    chosen = routes[0]
    gates = gating(modulated, router_weight[0], chosen)
    target = chosen * most + slots[0]
    place = target[..., None] == jnp.arange(experts * most, dtype=jnp.int32)
    occupied = jnp.any(place, axis=1).astype(jnp.bfloat16)
    buffer = jnp.einsum(
        "tr,td->rd", occupied, modulated, preferred_element_type=jnp.float32
    ).astype(jnp.bfloat16)
    mix_weights = jnp.sum(jnp.where(place, gates[..., None], jnp.float32(0.0)), axis=1)
    w_first = expert_in[0]
    w_second = expert_out[0]
    copies = jnp.broadcast_to(
        buffer.reshape(experts, 1, most, width), (experts, shards, most, width)
    )
    outgoing = copies.reshape(devices, most, width)
    received = lax.all_to_all(outgoing, "expert", split_axis=0, concat_axis=0, tiled=True)
    count = received.shape[1]
    hidden = jax.nn.gelu(
        jnp.dot(received.reshape(-1, width), w_first, preferred_element_type=jnp.float32),
        approximate=True,
    )
    partial_value = (
        jnp.dot(hidden.astype(jnp.bfloat16), w_second, preferred_element_type=jnp.float32)
        .astype(jnp.bfloat16)
        .reshape(devices, count, width)
    )
    returned = lax.all_to_all(partial_value, "expert", split_axis=0, concat_axis=0, tiled=True)
    combined = jnp.sum(returned.reshape(experts, shards, most, width).astype(jnp.float32), axis=1)
    mixture = jnp.dot(
        mix_weights,
        combined.reshape(experts * most, width),
        precision=lax.Precision.HIGHEST,
        preferred_element_type=jnp.float32,
    )
    updated = incoming.astype(jnp.float32) + (1.0 + mod[2]) * mixture
    return updated.astype(jnp.bfloat16)[None]


def body(states, routes, slots, timesteps, router_weight, *rest):
    quad = lax.axis_size("expert") == router_weight.shape[2] == 4
    chosen_body = quad_body if quad else general_body
    return chosen_body(states, routes, slots, timesteps, router_weight, *rest)


def solution(mesh):
    in_specs = (
        P("comp", ("groups", "expert"), None),
        P("comp", ("groups", "expert"), None),
        P("comp", ("groups", "expert"), None),
        P(("groups", "comp")),
        P("comp", None, None),
        P("comp", None, "expert"),
        P("comp", "expert", None),
        P(),
    )
    out_specs = P("comp", ("groups", "expert"), None)
    return jax.shard_map(body, mesh=mesh, in_specs=in_specs, out_specs=out_specs, check_vma=False)
```

```python
import functools

import jax
import jax.numpy as jnp
from jax import lax
from jax.experimental import pallas as pl
from jax.experimental.pallas import tpu as pltpu
from jax.sharding import PartitionSpec as P

MIB = 1024 * 1024
VMEM = pl.BlockSpec(memory_space=pltpu.VMEM)
ANY = pl.BlockSpec(memory_space=pl.ANY)
HBM = pl.BlockSpec(memory_space=pltpu.HBM)
PARAMS = pltpu.CompilerParams(vmem_limit_bytes=10 * MIB)


def shifted(block, axis, distance):
    devices = range(lax.axis_size(axis))
    route = [((i - distance) % len(devices), i) for i in devices]
    return lax.ppermute(block, axis, route)


def swapped(block, mask):
    return lax.ppermute(block, "expert", [(e, e ^ mask) for e in range(lax.axis_size("expert"))])


def advanced(block, mask):
    comps, experts = lax.axis_size("comp"), lax.axis_size("expert")
    route = [
        (c * experts + e, (c + 1) % comps * experts + (e ^ mask))
        for c in range(comps)
        for e in range(experts)
    ]
    return lax.ppermute(block, ("comp", "expert"), route)


def modulate(incoming, scale, shift):
    values = incoming.astype(jnp.float32)
    centred = values - jnp.mean(values, axis=-1, keepdims=True)
    spread = jnp.mean(centred * centred, axis=-1, keepdims=True)
    normed = centred * lax.rsqrt(spread + 1e-06)
    return (normed * (1.0 + scale) + shift).astype(jnp.bfloat16)


def slot_rows(target, mask, most):
    rows = lax.broadcasted_iota(jnp.int32, (most, target.shape[1]), 0) + mask * most
    hit = (rows == target[0:1, :]) | (rows == target[1:2, :])
    return jnp.where(hit, 1.0, 0.0).astype(jnp.bfloat16)


def select(rows, block):
    return jnp.dot(rows, block, preferred_element_type=jnp.float32).astype(jnp.bfloat16)


def gate_column(target, gates, mask, most):
    picked = (target >= mask * most) & (target < (mask + 1) * most)
    row = jnp.sum(jnp.where(picked, gates, 0.0), axis=0, keepdims=True)
    size = target.shape[1]
    places = (size, size)
    same = lax.broadcasted_iota(jnp.int32, places, 0) == lax.broadcasted_iota(jnp.int32, places, 1)
    return jnp.sum(jnp.where(same, row, 0.0), axis=1, keepdims=True)


def mixed(target, gates, mask, result):
    rows = slot_rows(target, mask, result.shape[0])
    spread = lax.dot_general(
        rows, result, (((0,), (0,)), ((), ())), preferred_element_type=jnp.float32
    )
    return gate_column(target, gates, mask, result.shape[0]) * spread


def tiles(size, step):
    return [(i, min(step, size - i)) for i in range(0, size, step)]


def first_layer(x, w1, hidden, ready=lambda index: None):
    for index, (start, size) in enumerate(tiles(w1.shape[1], 512)):
        ready(index)
        value = jnp.dot(x[...], w1[:, start:start + size], preferred_element_type=jnp.float32)
        hidden[:, start:start + size] = jax.nn.gelu(value, approximate=True).astype(jnp.bfloat16)


def second_layer(hidden, w2, columns, outs, ready=lambda index: None):
    pad = hidden.shape[0] // len(outs)
    for index, (start, size) in enumerate(tiles(columns[1] - columns[0], 512)):
        ready(index)
        part = w2[:, columns[0] + start:columns[0] + start + size]
        value = jnp.dot(hidden[...], part, preferred_element_type=jnp.float32)
        for i, out in enumerate(outs):
            rows = value[i * pad:i * pad + out.shape[0]]
            out[:, start:start + size] = rows.astype(jnp.bfloat16)


def sibling_kernel(source, ahead, target, out, out_source, out_target):
    out_target[...] = target[...]
    out[...] = select(slot_rows(ahead[...], 1, out.shape[0]), source[...])
    out_source[...] = source[...]


def source_kernel(mask, source, ahead, after, out):
    del after
    first = source.shape[1] - out.shape[1]
    out[...] = select(slot_rows(ahead[...], mask, out.shape[0]), source[:, first:])


def load_kernel(weight, after, out, sems):
    del after
    copies = [
        pltpu.make_async_copy(
            weight.at[:, pl.ds(start, size)], out.at[:, pl.ds(start, size)], sems.at[index]
        )
        for index, (start, size) in enumerate(tiles(weight.shape[1], 512))
    ]
    for copy in copies:
        copy.start()
    for copy in copies:
        copy.wait()


def relay_kernel(crossed, target, after, out_here, out_there):
    del after
    most = out_here.shape[0]
    out_here[...] = select(slot_rows(target[...], 2, most), crossed[...])
    out_there[...] = select(slot_rows(target[...], 3, most), crossed[...])


def gate_kernel(own, target, chosen, mod, router, out, gates):
    modulated = modulate(own[...], mod[0:1, :], mod[1:2, :])
    logits = lax.dot_general(
        router[...], modulated, (((1,), (1,)), ((), ())), preferred_element_type=jnp.float32
    )
    picked = jnp.zeros(chosen.shape, jnp.float32)
    for expert in range(router.shape[0]):
        picked += jnp.where(chosen[...] == expert, logits[expert:expert + 1, :], 0.0)
    sig = jax.nn.sigmoid(picked)
    gates[...] = sig / jnp.sum(sig, axis=0, keepdims=True)
    out[...] = select(slot_rows(target[...], 0, out.shape[0]), modulated)


def pack_gates(gates, rows):
    row = lax.broadcasted_iota(jnp.int32, (rows, gates.shape[1]), 0)
    packed = jnp.zeros(row.shape, jnp.float32)
    for index in range(3):
        piece = gates.astype(jnp.bfloat16).astype(jnp.float32)
        gates = gates - piece
        for k in range(2):
            packed = jnp.where(row == 2 * index + k, piece[k:k + 1, :], packed)
    return packed.astype(jnp.bfloat16)


def unpack_gates(packed):
    pieces = packed[0:16, :].astype(jnp.float32)
    return (pieces[0:2, :] + pieces[2:4, :]) + pieces[4:6, :]


def far_hidden(left, right, mod, w1, hidden, raw, x):
    most, cut = left.shape
    raw[:, 0:cut] = left[...].astype(jnp.float32)
    raw[:, cut:] = right[...].astype(jnp.float32)
    for start, size in tiles(most, 16):
        x[start:start + size, :] = modulate(raw[start:start + size, :], mod[0:1, :], mod[1:2, :])
    first_layer(x, w1, hidden)


def cross_kernel(left, right, mod, gates, w1, w2, out, hidden, raw, x):
    width = w2.shape[1]
    part = out.shape[1] - gates.shape[1]
    out[:, part:] = pack_gates(gates[...], out.shape[0])
    far_hidden(left, right, mod, w1, hidden, raw, x)
    second_layer(hidden, w2, (width - part, width), (out.at[:, 0:part],))


def far_kernel(
    left, right, mod, w1, w2, x_hidden, after, out_x, out_z, z_hidden, hidden, raw, x
):
    del after
    most, cut = left.shape
    pad = hidden.shape[0] // 2
    hidden[...] = jnp.zeros_like(hidden)
    hidden[0:most, :] = x_hidden[...]
    far_hidden(left, right, mod, w1, hidden.at[pad:pad + most, :], raw, x)
    z_hidden[...] = hidden[pad:pad + most, :]
    second_layer(hidden, w2, (0, out_x.shape[1]), (out_x, out_z))


def rest_kernel(hidden, w2, out):
    second_layer(hidden, w2, (w2.shape[1] - out.shape[1], w2.shape[1]), (out,))


def near_kernel(own, sib, mod, w1, w2, after, out_own, out_first, out_second, raw, x, hidden):
    del after
    most = own.shape[0]
    raw[0:most, :] = own[...].astype(jnp.float32)
    for start, size in tiles(most, 16):
        rows = modulate(sib[start:start + size, :], mod[0:1, :], mod[1:2, :])
        raw[most + start:most + start + size, :] = rows.astype(jnp.float32)
    x[...] = raw[...].astype(jnp.bfloat16)
    first_layer(x, w1, hidden)
    cut = out_first.shape[1]
    second_layer(hidden, w2, (0, cut), (out_own.at[:, 0:cut], out_first))
    second_layer(hidden, w2, (cut, w2.shape[1]), (out_own.at[:, cut:], out_second))


def copy_kernel(source, after, out):
    del after
    out[...] = source[...]


def joint_kernel(target, carried, here, there, after, out):
    del after
    gates = unpack_gates(carried[:, carried.shape[1] - target.shape[1]:])
    value = mixed(target[...], gates, 2, here[...])
    value += mixed(target[...], gates, 3, there[...])
    out[...] = value.astype(jnp.bfloat16)


def home_kernel(target, gates, y_own, y_x, y_z, out):
    part = y_z.shape[1]
    cut = y_own.shape[1] - part
    place, weight = target[...], gates[...]
    own = mixed(place, weight, 0, y_own[...])
    far = mixed(place, weight, 2, y_x[:, 0:part]) + mixed(place, weight, 3, y_z[...])
    out[:, 0:cut] = own[:, 0:cut]
    out[:, cut:] = own[:, cut:] + far


def add_kernel(incoming, mod, target, gates, mixture, y_first, y_second, out_left, out_right):
    place, weight = target[...], gates[...]
    cut = out_left.shape[1]
    first = mixed(place, weight, 1, y_first[...])
    second = mixed(place, weight, 1, y_second[...])
    scale = 1.0 + mod[2:3, :]
    near = jnp.concatenate([first, second], axis=1)
    total = incoming[...].astype(jnp.float32) + scale * (mixture[...] + near)
    out_left[...] = total[:, 0:cut]
    out_right[...] = total[:, cut:].astype(jnp.bfloat16)


def last_kernel(mod, left, right, joint, out):
    cut = joint.shape[1]
    value = left[...] + (1.0 + mod[2:3, 0:cut]) * joint[...].astype(jnp.float32)
    out[:, 0:cut] = value.astype(jnp.bfloat16)
    out[:, cut:] = right[...]


def cost(flops):
    return pl.CostEstimate(flops=flops, bytes_accessed=flops // 1024, transcendentals=0)


SHORT, LONG = cost(1 << 20), cost(1 << 37)


def padded(most):
    return -(-most // 16) * 16


def array(rows, columns, dtype=jnp.bfloat16):
    return jax.ShapeDtypeStruct((rows, columns), dtype)


def sibling_pass(source, ahead, target, most):
    return pl.pallas_call(
        sibling_kernel,
        out_shape=(
            array(most, source.shape[1]),
            array(*source.shape),
            array(*target.shape, target.dtype),
        ),
        in_specs=[VMEM] * 3,
        out_specs=(VMEM,) * 3,
        compiler_params=PARAMS,
        cost_estimate=SHORT,
    )(source, ahead, target)


def source_pass(mask, source, ahead, after, most, first):
    return pl.pallas_call(
        functools.partial(source_kernel, mask),
        out_shape=array(most, source.shape[1] - first),
        in_specs=[VMEM] * 2 + [ANY],
        out_specs=VMEM,
        compiler_params=PARAMS,
        cost_estimate=SHORT,
    )(source, ahead, after)


def load_pass(weight, after):
    loaded = pl.pallas_call(
        load_kernel,
        out_shape=pltpu.VMEM(weight.shape, weight.dtype),
        in_specs=[HBM, ANY],
        out_specs=VMEM,
        scratch_shapes=[pltpu.SemaphoreType.DMA((len(tiles(weight.shape[1], 512)),))],
        compiler_params=PARAMS,
        cost_estimate=SHORT,
    )(pltpu.with_memory_space_constraint(weight, pltpu.HBM), after)
    return pltpu.with_memory_space_constraint(loaded, pltpu.VMEM)


def relay_pass(crossed, target, after, most):
    part = array(most, crossed.shape[1])
    return pl.pallas_call(
        relay_kernel,
        out_shape=(part, part),
        in_specs=[VMEM] * 2 + [ANY],
        out_specs=(VMEM,) * 2,
        compiler_params=PARAMS,
        cost_estimate=SHORT,
    )(crossed, target, after)


def gate_pass(own, target, chosen, mod, router, most):
    return pl.pallas_call(
        gate_kernel,
        out_shape=(array(most, own.shape[1]), array(*chosen.shape, jnp.float32)),
        in_specs=[VMEM] * 5,
        out_specs=(VMEM,) * 2,
        compiler_params=PARAMS,
        cost_estimate=SHORT,
    )(own, target, chosen, mod, router)


def cross_pass(left, right, mod, gates, w1, w2, cut):
    most = left.shape[0]
    width, hid = w1.shape
    return pl.pallas_call(
        cross_kernel,
        out_shape=(array(most, width - cut + gates.shape[1]), array(most, hid)),
        in_specs=[VMEM] * 6,
        out_specs=(VMEM,) * 2,
        scratch_shapes=[
            pltpu.VMEM((most, width), jnp.float32),
            pltpu.VMEM((most, width), jnp.bfloat16),
        ],
        compiler_params=PARAMS,
        cost_estimate=SHORT,
    )(left, right, mod, gates, w1, w2)


def far_pass(left, right, mod, w1, w2, x_hidden, after, cut):
    most = left.shape[0]
    width, hid = w1.shape
    return pl.pallas_call(
        far_kernel,
        out_shape=(array(most, cut), array(most, cut), array(most, hid)),
        in_specs=[VMEM] * 6 + [ANY],
        out_specs=(VMEM,) * 3,
        scratch_shapes=[
            pltpu.VMEM((2 * padded(most), hid), jnp.bfloat16),
            pltpu.VMEM((most, width), jnp.float32),
            pltpu.VMEM((most, width), jnp.bfloat16),
        ],
        compiler_params=PARAMS,
        cost_estimate=SHORT,
    )(left, right, mod, w1, w2, x_hidden, after)


def rest_pass(hidden, w2, part):
    return pl.pallas_call(
        rest_kernel,
        out_shape=array(hidden.shape[0], part),
        in_specs=[VMEM] * 2,
        out_specs=VMEM,
        compiler_params=PARAMS,
        cost_estimate=SHORT,
    )(hidden, w2)


def near_pass(own, sib, mod, w1, w2, after, cut):
    most, width = sib.shape
    return pl.pallas_call(
        near_kernel,
        out_shape=(array(most, width), array(most, cut), array(most, width - cut)),
        in_specs=[VMEM] * 5 + [ANY],
        out_specs=(VMEM,) * 3,
        scratch_shapes=[
            pltpu.VMEM((2 * most, width), jnp.float32),
            pltpu.VMEM((2 * most, width), jnp.bfloat16),
            pltpu.VMEM((2 * most, w1.shape[1]), jnp.bfloat16),
        ],
        compiler_params=PARAMS,
        cost_estimate=SHORT,
    )(own, sib, mod, w1, w2, after)


def copy_pass(source, after):
    return pl.pallas_call(
        copy_kernel,
        out_shape=array(*source.shape),
        in_specs=[VMEM, ANY],
        out_specs=VMEM,
        compiler_params=PARAMS,
        cost_estimate=SHORT,
    )(source, after)


def joint_pass(target, carried, here, there, after):
    return pl.pallas_call(
        joint_kernel,
        out_shape=array(target.shape[1], here.shape[1]),
        in_specs=[VMEM] * 4 + [ANY],
        out_specs=VMEM,
        compiler_params=PARAMS,
        cost_estimate=SHORT,
    )(target, carried, here, there, after)


def home_pass(target, gates, y_own, y_x, y_z):
    return pl.pallas_call(
        home_kernel,
        out_shape=array(target.shape[1], y_own.shape[1], jnp.float32),
        in_specs=[VMEM] * 5,
        out_specs=VMEM,
        compiler_params=PARAMS,
        cost_estimate=LONG,
    )(target, gates, y_own, y_x, y_z)


def add_pass(incoming, mod, target, gates, mixture, y_first, y_second, cut):
    tokens, width = incoming.shape
    return pl.pallas_call(
        add_kernel,
        out_shape=(array(tokens, cut, jnp.float32), array(tokens, width - cut)),
        in_specs=[VMEM] * 7,
        out_specs=(VMEM,) * 2,
        compiler_params=PARAMS,
        cost_estimate=SHORT,
    )(incoming, mod, target, gates, mixture, y_first, y_second)


def last_pass(mod, left, right, joint):
    return pl.pallas_call(
        last_kernel,
        out_shape=array(left.shape[0], left.shape[1] + right.shape[1]),
        in_specs=[VMEM] * 4,
        out_specs=VMEM,
        compiler_params=PARAMS,
        cost_estimate=SHORT,
    )(mod, left, right, joint)


def quad_body(states, routes, slots, timesteps, router_weight, expert_in, expert_out, modulation):
    source = states[0]
    width = source.shape[1]
    most = 3 * source.shape[0] // 4
    cut = width // 256 * 128
    back_cut = cut
    sib_cut = cut + 256
    here = lax.axis_index("expert")
    chosen = routes[0].T
    target = (chosen ^ here) * most + slots[0].T
    ahead = shifted(target, "comp", -1)
    crossed = advanced(source[:, :cut], 2)
    mod = modulation[timesteps[0]].astype(jnp.float32)

    s_source, same, same_target = sibling_pass(source, ahead, target, most)
    x_target = swapped(same_target, 2)
    incoming = shifted(same, "comp", 1)
    sib = advanced(s_source, 1)
    w1 = load_pass(expert_in[0], s_source)
    far_x = advanced(source_pass(2, source, ahead, w1, most, cut), 2)
    own, gates = gate_pass(incoming, target, chosen, mod, router_weight[0].T, most)

    near_x, passed = relay_pass(crossed, x_target, w1, most)
    near_z = swapped(passed, 1)
    z_source = source_pass(3, source, ahead, passed, most, cut)
    far_z = advanced(z_source, 3)
    w2 = load_pass(expert_out[0], z_source)
    x_right, x_hidden = cross_pass(near_x, far_x, mod, gates, w1, w2, back_cut)
    back_x = swapped(x_right, 2)
    y_own, s_first, s_second = near_pass(own, sib, mod, w1, w2, x_right, sib_cut)
    back_first = swapped(s_first, 1)
    x_left, z_left, z_hidden = far_pass(
        near_z, far_z, mod, w1, w2, x_hidden, x_hidden, back_cut
    )
    lent = swapped(z_left, 1)
    back_z = swapped(rest_pass(z_hidden, w2, width - back_cut), 3)
    joint = joint_pass(x_target, back_x, x_left, lent, back_first)
    back_second = swapped(copy_pass(s_second, joint), 1)
    joint = swapped(joint, 2)
    mixture = home_pass(target, gates, y_own, back_x, back_z)
    left, right = add_pass(
        incoming, mod, target, gates, mixture, back_first, back_second, back_cut
    )
    return last_pass(mod, left, right, joint)[None]


def gating(modulated, weight, chosen):
    logits = jnp.dot(modulated, weight, preferred_element_type=jnp.float32)
    picks = chosen[..., None] == jnp.arange(weight.shape[1], dtype=jnp.int32)
    selected = jnp.sum(jnp.where(picks, logits[:, None, :], jnp.float32(0.0)), axis=-1)
    sig = jax.nn.sigmoid(selected)
    return sig / jnp.sum(sig, axis=1, keepdims=True)


def general_body(states, routes, slots, timesteps, router_weight, expert_in, expert_out, modulation):
    devices = lax.axis_size("expert")
    tokens_here = states.shape[1]
    width = states.shape[2]
    experts = router_weight.shape[2]
    shards = devices // experts
    most = 3 * tokens_here // 4
    incoming = shifted(states[0], "comp", 1)
    mod = modulation[timesteps[0]].astype(jnp.float32)
    modulated = modulate(incoming, mod[0], mod[1])
    chosen = routes[0]
    gates = gating(modulated, router_weight[0], chosen)
    target = chosen * most + slots[0]
    place = target[..., None] == jnp.arange(experts * most, dtype=jnp.int32)
    occupied = jnp.any(place, axis=1).astype(jnp.bfloat16)
    buffer = jnp.einsum(
        "tr,td->rd", occupied, modulated, preferred_element_type=jnp.float32
    ).astype(jnp.bfloat16)
    mix_weights = jnp.sum(jnp.where(place, gates[..., None], jnp.float32(0.0)), axis=1)
    w_first = expert_in[0]
    w_second = expert_out[0]
    copies = jnp.broadcast_to(
        buffer.reshape(experts, 1, most, width), (experts, shards, most, width)
    )
    outgoing = copies.reshape(devices, most, width)
    received = lax.all_to_all(outgoing, "expert", split_axis=0, concat_axis=0, tiled=True)
    count = received.shape[1]
    hidden = jax.nn.gelu(
        jnp.dot(received.reshape(-1, width), w_first, preferred_element_type=jnp.float32),
        approximate=True,
    )
    partial_value = (
        jnp.dot(hidden.astype(jnp.bfloat16), w_second, preferred_element_type=jnp.float32)
        .astype(jnp.bfloat16)
        .reshape(devices, count, width)
    )
    returned = lax.all_to_all(partial_value, "expert", split_axis=0, concat_axis=0, tiled=True)
    combined = jnp.sum(returned.reshape(experts, shards, most, width).astype(jnp.float32), axis=1)
    mixture = jnp.dot(
        mix_weights,
        combined.reshape(experts * most, width),
        precision=lax.Precision.HIGHEST,
        preferred_element_type=jnp.float32,
    )
    updated = incoming.astype(jnp.float32) + (1.0 + mod[2]) * mixture
    return updated.astype(jnp.bfloat16)[None]


def body(states, routes, slots, timesteps, router_weight, *rest):
    quad = lax.axis_size("expert") == router_weight.shape[2] == 4
    chosen_body = quad_body if quad else general_body
    return chosen_body(states, routes, slots, timesteps, router_weight, *rest)


def solution(mesh):
    in_specs = (
        P("comp", ("groups", "expert"), None),
        P("comp", ("groups", "expert"), None),
        P("comp", ("groups", "expert"), None),
        P(("groups", "comp")),
        P("comp", None, None),
        P("comp", None, "expert"),
        P("comp", "expert", None),
        P(),
    )
    out_specs = P("comp", ("groups", "expert"), None)
    return jax.shard_map(body, mesh=mesh, in_specs=in_specs, out_specs=out_specs, check_vma=False)
```
